768 devices in a mesh: row: 16 (over x_lo, y), col: 48 (over x_hi, z, core).
Axes of the slice: x: 4 (x_hi: 2, x_lo: 2; x = x_hi * 2 + x_lo), y: 8, z: 12, core: 2. Of those that a mesh axis runs over, the one named last changes fastest.
Arguments:
- features: bfloat16 [98304, 128], P(('row', 'col')), may hold values from -6 to 6
- node_scale: bfloat16 [98304], P(('row', 'col')), may hold values from 0.099609375 to 0.29882812
- weight: bfloat16 [128, 256], replicated, may hold values from -0.5 to 0.5
- bias: float32 [256], replicated, may hold values from -3 to 3
- block_rows: int32 [16, 48, 16], P('row', 'col'), may hold values from 0 to 47, as said below
- block_cols: int32 [16, 48, 16], P('row', 'col'), may hold values from 0 to 15
- block_masks: int32 [16, 48, 16, 128, 128], P('row', 'col'), may hold values from 0 to 1, as said below
- out_grad: bfloat16 [98304, 256], P(('row', 'col')), may hold values from -6 to 6
Outputs:
- hidden: bfloat16 [98304, 256], P(('row', 'col'))
- grad_features: bfloat16 [98304, 128], P(('row', 'col'))
- grad_weight: float32 [128, 256], replicated
- grad_bias: float32 [256], replicated
The draws below stay inside these ranges and needn't reach their ends.
Inputs may be any that keep to these rules, and one draw needn't show every extreme that they name: `block_rows`: on each device, slot s names entry s % 48 of an ordering of the tile's 48 block rows, so a block row repeats only after all have been named; repeated blocks add their edges. `block_masks`: on each device the slots that hold edges come first, at least 8 of them, and the rest are all zero; at least one device has edges in all 16 slots.
All inputs are finite; a program needn't handle non-finite values.
Results may differ from the reference program's by a relative error of at most 0.007.
Values may be sent and summed in bfloat16 or wider, within the bound.
A program may use at most 32 MiB of HBM per device.

```python
import math
import jax
import jax.numpy as jnp
from jax import lax

FIN = 128
HID = 256
BLOCK = 128
ROWS_DEV = 128
NB = 16
NODES = 98304
BCOLS = 16
N_ROW = 16
N_COL = 48


def draw_block_rows(key, part):
    key = jax.random.fold_in(key, 23)
    device_count = N_ROW * N_COL
    brows = N_COL * ROWS_DEV // BLOCK
    keys = jax.random.split(key, device_count)
    orders = jax.vmap(lambda one_key: jax.random.permutation(one_key, brows))(keys)
    picks = jnp.arange(NB, dtype=jnp.int32) % brows
    rows = orders[:, picks].astype(jnp.int32)
    return rows.reshape(N_ROW, N_COL, NB)


def draw_block_masks(key, part):
    key = jax.random.fold_in(key, 11)
    key_live, key_full, key_edges = jax.random.split(key, 3)
    device_count = N_ROW * N_COL
    live = jax.random.randint(key_live, (device_count,), max(NB // 2, 1), NB + 1)
    full_device = jax.random.randint(key_full, (), 0, device_count)
    live = jnp.where(jnp.arange(device_count) == full_device, NB, live)
    alive = jnp.arange(NB)[None, :] < live[:, None]
    edges = jax.random.randint(key_edges, (device_count, NB, BLOCK, BLOCK), 0, 8) == 0
    masks = jnp.logical_and(edges, alive[:, :, None, None]).astype(jnp.int32)
    return masks.reshape(N_ROW, N_COL, NB, BLOCK, BLOCK)


def touch_ends(result, own_key, low, largest):
    spot = [jax.random.randint(jax.random.fold_in(own_key, axis), (), 0, length) for axis, length in enumerate(result.shape)]
    widest = result.shape.index(max(result.shape))
    neighbour = spot[:widest] + [(spot[widest] + 1) % result.shape[widest]] + spot[widest + 1:]
    return result.at[tuple(spot)].set(low).at[tuple(neighbour)].set(largest)


def level_of(key, extent, shards, low, top_value):
    level, own = 1.0, jax.random.fold_in(key, 6)
    for position, blocks in shards:
        draws = jnp.exp(jax.random.uniform(jax.random.fold_in(own, position), (blocks,), jnp.float32, low / len(shards), top_value / len(shards)))
        level = level * jnp.repeat(draws, extent[position] // blocks).reshape([-1 if axis == position else 1 for axis in range(len(extent))])
    return level


def bell_draw(key, extent, deviation, bound, shards=(), kind=jnp.bfloat16):
    values = jax.random.normal(key, extent, jnp.float32) * deviation
    if len(shards) > 0:
        values = level_of(key, extent, shards, -0.22, 0.18) * values
    return jnp.clip(values, min=-bound, max=bound).astype(kind)


def setup_inputs(seed: int = 0) -> dict:
    splits = jax.random.split(jax.random.key(seed), 9)
    return {
        "features": bell_draw(splits[0], (NODES, FIN), 1.0, 6.0, ((0, 768),)),
        "node_scale": jnp.clip(jnp.exp(math.log(0.29882812) - 1.0986123 * jax.random.uniform(splits[1], (NODES,), jnp.float32) ** level_of(splits[1], (NODES,), ((0, 768),), -0.2, 0.2)), 0.099609375, 0.29882812).astype(jnp.bfloat16),
        "weight": bell_draw(splits[2], (FIN, HID), FIN ** -0.5, 0.5),
        "bias": bell_draw(splits[3], (HID,), 0.5, 3.0, (), jnp.float32),
        "block_rows": draw_block_rows(jax.random.fold_in(splits[8], 71), 0),
        "block_cols": touch_ends(jax.random.randint(splits[5], (N_ROW, N_COL, NB), 0, BCOLS), jax.random.fold_in(splits[5], 1), 0, BCOLS - 1).astype(jnp.int32),
        "block_masks": draw_block_masks(jax.random.fold_in(splits[8], 71), 0),
        "out_grad": bell_draw(splits[7], (NODES, HID), 1.0, 6.0, ((0, 768),)),
    }


def activation(value):
    return jax.nn.gelu(value, approximate=True)

def place_blocks(contrib, coords, total_blocks):
    selector = (coords[None, :] == jnp.arange(total_blocks, dtype=jnp.int32)[:, None]).astype(jnp.float32)
    return jnp.einsum('bs,sif->bif', selector, contrib.astype(jnp.float32), precision=lax.Precision.HIGHEST)

def reference(features, node_scale, weight, bias, block_rows, block_cols, block_masks, out_grad):
    feature_width = features.shape[1]
    tile_rows = N_COL * ROWS_DEV
    tile_cols = N_ROW * ROWS_DEV
    scale_col = node_scale.astype(jnp.float32)[:, None]
    scaled = (scale_col * features.astype(jnp.float32)).astype(jnp.bfloat16)
    grid = scaled.reshape(N_ROW, N_COL, ROWS_DEV, feature_width)

    def forward_step(total, index):
        row_index = (index // N_COL).astype(jnp.int32)
        col_index = (index % N_COL).astype(jnp.int32)
        column_group = jnp.take(grid, col_index, axis=1).reshape(tile_cols // BLOCK, BLOCK, feature_width)
        masks = block_masks[row_index, col_index].astype(jnp.float32)
        picked = column_group[block_cols[row_index, col_index]].astype(jnp.float32)
        products = jnp.einsum('sij,sjf->sif', masks, picked, precision=lax.Precision.HIGHEST)
        partial_value = place_blocks(products, block_rows[row_index, col_index], tile_rows // BLOCK).reshape(tile_rows, feature_width)
        offset = (row_index * tile_rows).astype(jnp.int32)
        current = lax.dynamic_slice_in_dim(total, offset, tile_rows, 0)
        return (lax.dynamic_update_slice_in_dim(total, current + partial_value, offset, 0), None)
    indices = jnp.arange(N_ROW * N_COL, dtype=jnp.int32)
    start = jnp.zeros((N_ROW * N_COL * ROWS_DEV, feature_width), jnp.float32)
    summed, unused = lax.scan(forward_step, start, indices)
    aggregated = (scale_col * summed).astype(jnp.bfloat16)
    preact = jnp.dot(aggregated, weight, preferred_element_type=jnp.float32) + bias
    active, pullback = jax.vjp(activation, preact)
    hidden = active.astype(jnp.bfloat16)
    grad_pre = pullback(out_grad.astype(jnp.float32))[0].astype(jnp.bfloat16)
    grad_weight = jnp.dot(aggregated.T, grad_pre, preferred_element_type=jnp.float32)
    grad_bias = lax.optimization_barrier(jnp.sum(grad_pre.astype(jnp.float32), axis=0))
    message = (scale_col * jnp.dot(grad_pre, weight.T, preferred_element_type=jnp.float32)).astype(jnp.bfloat16)
    message_grid = message.reshape(N_ROW, tile_rows // BLOCK, BLOCK, feature_width)

    def backward_step(total, index):
        row_index = (index // N_COL).astype(jnp.int32)
        col_index = (index % N_COL).astype(jnp.int32)
        row_group = jnp.take(message_grid, row_index, axis=0)
        masks = block_masks[row_index, col_index].astype(jnp.float32)
        chosen = row_group[block_rows[row_index, col_index]].astype(jnp.float32)
        back_terms = jnp.einsum('sij,sif->sjf', masks, chosen, precision=lax.Precision.HIGHEST)
        partial_value = place_blocks(back_terms, block_cols[row_index, col_index], tile_cols // BLOCK).reshape(N_ROW, ROWS_DEV, feature_width)
        return (total.at[:, col_index].add(partial_value), None)
    back_start = jnp.zeros((N_ROW, N_COL, ROWS_DEV, feature_width), jnp.float32)
    back_total, unused_back = lax.scan(backward_step, back_start, indices)
    grad_features = (scale_col * back_total.reshape(-1, feature_width)).astype(jnp.bfloat16)
    return (hidden, grad_features, grad_weight, grad_bias)
```

```python
import functools
import math

import jax
import jax.numpy as jnp
from jax import lax
from jax.experimental import pallas as pl
from jax.experimental.pallas import tpu as pltpu
from jax.sharding import PartitionSpec as P

MESH = pl.DeviceIdType.MESH
UP, DOWN = 0, 1


def kernel(
    ny, nz,
    table, scale_ref, features_ref, weight_ref, bias_ref, masks_ref, cotangent_ref,
    hidden_ref, grad_features_ref, grad_weight_ref, grad_bias_ref,
    masks, masks_t, gathered, products, pair_out, pair_in, ring_out, ring_in, edge_out, edge_in,
    messages, back, back_out, back_in, back_edge_out, back_edge_in,
    parts, parts_in, halves, y_in, x_terms, z_terms, finals,
    send_sems, recv_sems,
):
    f32, bf16 = jnp.float32, jnp.bfloat16
    slots = masks.shape[0]
    row, col = lax.axis_index("row"), lax.axis_index("col")
    xl, y = row // ny, row % ny
    xh, z, core = col // (2 * nz), (col % (2 * nz)) // 2, col % 2

    def row_of(x_lo, y_at):
        return x_lo * ny + y_at

    def col_of(x_hi, z_at, core_at):
        return x_hi * (2 * nz) + z_at * 2 + core_at

    sibling = (row, col_of(xh, z, 1 - core))
    lo_partner = (row_of(1 - xl, y), col)
    hi_partner = (row, col_of(1 - xh, z, core))
    far_partner = (row_of(1 - xl, y), col_of(1 - xh, z, core))
    y_peers = [(row_of(xl, (y + j) % ny), col) for j in range(1, ny)]
    z_peers = [(row, col_of(xh, (z + j) % nz, core)) for j in range(1, nz)]

    barrier = pltpu.get_barrier_semaphore()
    everyone = [sibling, lo_partner, hi_partner, far_partner] + y_peers + z_peers
    for peer in everyone:
        pl.semaphore_signal(barrier, inc=1, device_id=peer, device_id_type=MESH)

    started = []

    def send(src, dst, peer):
        number = len(started)
        copy = pltpu.make_async_remote_copy(
            src_ref=src, dst_ref=dst, send_sem=send_sems.at[number], recv_sem=recv_sems.at[number],
            device_id=peer, device_id_type=MESH,
        )
        started.append(copy)
        copy.start()
        return copy

    scale = jnp.broadcast_to(scale_ref[...].astype(f32), (128, 128)).T
    gathered[row] = (scale * features_ref[...].astype(f32)).astype(bf16)
    pl.semaphore_wait(barrier, len(everyone))

    def gather(buffer, index, place, count, partner, up, down, arrived, hook):
        half = count // 2
        mine = buffer.at[index(0, place)]
        swap = send(mine, mine, partner)
        arrived(index(0, place))
        copies = {}
        for hop in range(1, half + 2):
            for piece in (0, 1):
                if hop == 1 and piece == 1:
                    swap.wait_recv()
                    arrived(index(1, place))
                for way in (UP, DOWN):
                    back_by = (place - (hop - 1)) % count if way == UP else (place + (hop - 1)) % count
                    if (way, hop - 1, piece) in copies:
                        copies[way, hop - 1, piece].wait_recv()
                        arrived(index(piece, back_by))
                    if hop < half or (hop == half and (way == UP) == (piece == 0)):
                        block = buffer.at[index(piece, back_by)]
                        copies[way, hop, piece] = send(block, block, up if way == UP else down)
            hook(hop)

    def reduce(own, place, count, partner, up, down, outs, ins, edge_send, edge_recv, ready, hook):
        half = count // 2
        copies = {}

        def value(way, piece, distance, dest, slot):
            total = own(piece, dest, slot)
            if (way, piece, distance + 1) in copies:
                copies[way, piece, distance + 1][0].wait_recv()
                total = total + ins[copies[way, piece, distance + 1][1]].astype(f32)
            return total

        number = 0
        for distance in range(half, 0, -1):
            ready(distance)
            for piece in (0, 1):
                for way in (UP, DOWN):
                    if distance == half and (way == UP) != (piece == 0):
                        continue
                    dest = (place + distance) % count if way == UP else (place - distance) % count
                    outs[number] = value(way, piece, distance, dest, number).astype(bf16)
                    copies[way, piece, distance] = (
                        send(outs.at[number], ins.at[number], up if way == UP else down), number
                    )
                    number += 1
            hook(distance)
        ready(0)

        def arrived_sum(piece):
            total = own(piece, place, number + piece)
            for way in (UP, DOWN):
                if (way, piece, 1) in copies:
                    copies[way, piece, 1][0].wait_recv()
                    total = total + ins[copies[way, piece, 1][1]].astype(f32)
            return total

        edge_send[...] = arrived_sum(1).astype(bf16)
        edge = send(edge_send, edge_recv, partner)
        mine = arrived_sum(0)
        hook(0)
        edge.wait_recv()
        return mine + edge_recv[...].astype(f32)

    def no_hook(step):
        return None

    def row_index(piece, y_at):
        return row_of(xl if piece == 0 else 1 - xl, y_at)

    def prepare(step):
        if step != 1:
            return

        def body(slot, carry):
            block = masks_ref[slot].astype(f32)
            masks[slot] = block.astype(bf16)
            masks_t[slot] = block.T.astype(bf16)
            return carry

        lax.fori_loop(0, slots, body, 0)
        products[slots] = jnp.zeros((128, 128), f32)
        back[slots] = jnp.zeros((128, 128), f32)

    gather(gathered, row_index, y, ny, lo_partner, y_peers[0], y_peers[ny - 2], no_hook, prepare)

    for slot in range(slots):
        products[slot] = jnp.dot(
            masks[slot], gathered[table[slot]], preferred_element_type=f32
        )

    def term(piece, z_at, core_at):
        x_hi = xh if piece == 0 else 1 - xh
        return products[table[4 * slots + col_of(x_hi, z_at, core_at)]]

    half_z = nz // 2
    pair_copies = {}
    number = 0
    for distance in range(half_z, -1, -1):
        first = number
        for piece in (0, 1):
            for way in (UP, DOWN):
                if distance in (half_z, 0) and (way == UP) != (piece == 0):
                    continue
                dest = (z + distance) % nz if way == UP else (z - distance) % nz
                pair_out[number] = term(piece, dest, 1 - core).astype(bf16)
                number += 1
        span = pl.ds(first, number - first)
        pair_copies[distance] = send(pair_out.at[span], pair_in.at[span], sibling)

    def own_forward(piece, dest, slot):
        return term(piece, dest, core) + pair_in[slot].astype(f32)

    summed = reduce(
        own_forward, z, nz, hi_partner, z_peers[0], z_peers[nz - 2], ring_out, ring_in,
        edge_out, edge_in, lambda distance: pair_copies[distance].wait_recv(), no_hook,
    )

    aggregated = (scale * summed).astype(bf16)
    weight = weight_ref[...]
    preact = jnp.dot(aggregated, weight, preferred_element_type=f32) + bias_ref[...]
    root = math.sqrt(2.0 / math.pi)
    square = preact * preact
    slope = jnp.tanh(root * (preact + 0.044715 * (square * preact)))
    cdf = 0.5 * (1.0 + slope)
    derivative = cdf + preact * (0.5 * (1.0 - slope * slope) * (root * (1.0 + 0.134145 * square)))
    grad_pre = (cotangent_ref[...].astype(f32) * derivative).astype(bf16)
    message = scale * lax.dot_general(
        grad_pre, weight, (((1,), (1,)), ((), ())), preferred_element_type=f32
    )

    def column_index(piece, z_at):
        return (core * 2 + (xh if piece == 0 else 1 - xh)) * nz + z_at

    messages[column_index(0, z)] = message.astype(bf16)

    chunk = parts.shape[2]
    state = {}

    def weight_start():
        hidden_ref[...] = (preact * cdf).astype(bf16)
        weight_part = lax.dot_general(
            aggregated, grad_pre, (((0,), (0,)), ((), ())), preferred_element_type=f32
        )
        bias_part = jnp.sum(grad_pre.astype(f32), axis=0, keepdims=True)
        lines = lax.broadcasted_iota(jnp.int32, (chunk, 128), 0)
        bias_tile = jnp.where(
            lines == 0, bias_part[:, :128], jnp.where(lines == 1, bias_part[:, 128:], 0.0)
        )
        for core_at in (0, 1):
            for y_at in range(ny):
                first = (core_at * ny + y_at) * chunk
                parts[core_at, y_at, :, :256] = weight_part[first : first + chunk]
                parts[core_at, y_at, :, 256:] = bias_tile
        state["pair"] = send(parts.at[1 - core], parts_in, sibling)

    def weight_y():
        state["pair"].wait_recv()
        halves[...] = parts[core] + parts_in[...]
        state["y"] = [
            send(halves.at[(y + j) % ny], y_in.at[j - 1], y_peers[j - 1]) for j in range(1, ny)
        ]

    def weight_x():
        total = halves[y]
        for j, copy in enumerate(state["y"]):
            copy.wait_recv()
            total = total + y_in[j]
        x_at = xh * 2 + xl
        x_terms[x_at] = total
        state["x"] = [
            send(x_terms.at[x_at], x_terms.at[x_at], peer)
            for peer in (lo_partner, hi_partner, far_partner)
        ]

    def weight_z():
        for copy in state["x"]:
            copy.wait_recv()
        z_terms[z] = (x_terms[0] + x_terms[1]) + (x_terms[2] + x_terms[3])
        state["z"] = [send(z_terms.at[z], z_terms.at[z], peer) for peer in z_peers]

    def weight_spread():
        for copy in state["z"]:
            copy.wait_recv()
        total = z_terms[0]
        for j in range(1, nz):
            total = total + z_terms[j]
        finals[core, y] = total
        state["spread"] = [
            send(finals.at[core, y], finals.at[core, y], peer) for peer in y_peers
        ]

    def weight_pair():
        for copy in state["spread"]:
            copy.wait_recv()
        state["last"] = send(finals.at[core], finals.at[core], sibling)

    def weight_store():
        state["last"].wait_recv()
        for core_at in (0, 1):
            for y_at in range(ny):
                first = (core_at * ny + y_at) * chunk
                grad_weight_ref[first : first + chunk, :] = finals[core_at, y_at, :, :256]
        grad_bias_ref[...] = finals[0, 0, 0:2, 256:]

    shared = []

    def share(index):
        shared.append(send(messages.at[index], messages.at[index], sibling))

    gather_steps = {1: weight_start, 3: weight_y, 5: weight_x, half_z + 1: weight_z}

    def gather_hook(step):
        if step in gather_steps:
            gather_steps[step]()

    gather(messages, column_index, z, nz, hi_partner, z_peers[0], z_peers[nz - 2], share, gather_hook)
    for copy in shared:
        copy.wait_recv()

    for slot in range(slots):
        product = jnp.dot(
            masks_t[slot], messages[table[slots + slot]], preferred_element_type=f32
        )
        back[slot] = product + back[table[2 * slots + slot]]

    def own_backward(piece, dest, slot):
        return back[table[3 * slots + row_index(piece, dest)]]

    reduce_steps = {2: weight_spread, 0: weight_pair}

    def reduce_hook(step):
        if step in reduce_steps:
            reduce_steps[step]()

    summed_back = reduce(
        own_backward, y, ny, lo_partner, y_peers[0], y_peers[ny - 2], back_out, back_in,
        back_edge_out, back_edge_in, no_hook, reduce_hook,
    )
    grad_features_ref[...] = (scale * summed_back).astype(bf16)
    weight_store()
    for copy in started:
        copy.wait_send()


def copies_of(ny, nz):
    def one_way(count):
        return 2 * (count - 1)

    gathers = (1 + one_way(ny)) + (1 + one_way(nz) + 2 * nz)
    reduces = (nz // 2 + 1) + (one_way(nz) + 1) + (one_way(ny) + 1)
    weights = 1 + (ny - 1) + 3 + (nz - 1) + (ny - 1) + 1
    return gathers + reduces + weights


def on_device(features, node_scale, weight, bias, block_rows, block_cols, block_masks, out_grad):
    ny, nz = lax.axis_size("row") // 2, lax.axis_size("col") // 4
    slots = block_masks.shape[2]
    row_ids, col_ids = block_rows.reshape(slots), block_cols.reshape(slots)
    numbers = jnp.arange(slots, dtype=jnp.int32)

    def named(match):
        found = jnp.max(jnp.where(match, numbers[None, :], -1), axis=1)
        return jnp.where(found < 0, slots, found)

    message_ids = (row_ids % 2) * (2 * nz) + (row_ids // (2 * nz)) * nz + (row_ids % (2 * nz)) // 2
    earlier = named((col_ids[:, None] == col_ids[None, :]) & (numbers[None, :] < numbers[:, None]))
    last = named(jnp.arange(2 * ny, dtype=jnp.int32)[:, None] == col_ids[None, :])
    owners = named(jnp.arange(4 * nz, dtype=jnp.int32)[:, None] == row_ids[None, :])
    pad = jnp.zeros((slots - 2 * ny,), jnp.int32)
    table = jnp.concatenate([col_ids, message_ids, earlier, last, pad, owners])

    bf16, f32 = jnp.bfloat16, jnp.float32
    chunk = weight.shape[0] // (2 * ny)
    block = (128, 128)
    vmem = pl.BlockSpec(memory_space=pltpu.VMEM)
    copies = copies_of(ny, nz)
    hidden, grad_features, grad_weight, grad_bias = pl.pallas_call(
        functools.partial(kernel, ny, nz),
        out_shape=(
            jax.ShapeDtypeStruct((128, 256), bf16),
            jax.ShapeDtypeStruct(block, bf16),
            jax.ShapeDtypeStruct((128, 256), f32),
            jax.ShapeDtypeStruct((2, 128), f32),
        ),
        in_specs=[pl.BlockSpec(memory_space=pltpu.SMEM)] + [vmem] * 6,
        out_specs=(vmem,) * 4,
        scratch_shapes=[
            pltpu.VMEM((slots,) + block, bf16),
            pltpu.VMEM((slots,) + block, bf16),
            pltpu.VMEM((2 * ny,) + block, bf16),
            pltpu.VMEM((slots + 1,) + block, f32),
            pltpu.VMEM((2 * nz,) + block, bf16),
            pltpu.VMEM((2 * nz,) + block, bf16),
            pltpu.VMEM((2 * nz - 2,) + block, bf16),
            pltpu.VMEM((2 * nz - 2,) + block, bf16),
            pltpu.VMEM(block, bf16),
            pltpu.VMEM(block, bf16),
            pltpu.VMEM((4 * nz,) + block, bf16),
            pltpu.VMEM((slots + 1,) + block, f32),
            pltpu.VMEM((2 * ny - 2,) + block, bf16),
            pltpu.VMEM((2 * ny - 2,) + block, bf16),
            pltpu.VMEM(block, bf16),
            pltpu.VMEM(block, bf16),
            pltpu.VMEM((2, ny, chunk, 384), f32),
            pltpu.VMEM((ny, chunk, 384), f32),
            pltpu.VMEM((ny, chunk, 384), f32),
            pltpu.VMEM((ny - 1, chunk, 384), f32),
            pltpu.VMEM((4, chunk, 384), f32),
            pltpu.VMEM((nz, chunk, 384), f32),
            pltpu.VMEM((2, ny, chunk, 384), f32),
            pltpu.SemaphoreType.DMA((copies,)),
            pltpu.SemaphoreType.DMA((copies,)),
        ],
        compiler_params=pltpu.CompilerParams(
            collective_id=0, has_side_effects=True, vmem_limit_bytes=40 * 1024 * 1024
        ),
        cost_estimate=pl.CostEstimate(
            flops=200_000_000, bytes_accessed=2_000_000, transcendentals=32768
        ),
    )(
        table, node_scale.reshape(1, 128), features, weight, bias.reshape(1, 256),
        block_masks.reshape(slots, 128, 128), out_grad,
    )
    return hidden, grad_features, grad_weight, grad_bias.reshape(256)


def solution(mesh):
    return jax.shard_map(
        on_device,
        mesh=mesh,
        in_specs=(
            P(("row", "col"), None),
            P(("row", "col")),
            P(),
            P(),
            P("row", "col", None),
            P("row", "col", None),
            P("row", "col", None, None, None),
            P(("row", "col"), None),
        ),
        out_specs=(P(("row", "col"), None), P(("row", "col"), None), P(), P()),
        check_vma=False,
    )
```

```python
import functools
import math

import jax
import jax.numpy as jnp
from jax import lax
from jax.experimental import pallas as pl
from jax.experimental.pallas import tpu as pltpu
from jax.sharding import PartitionSpec as P

MESH = pl.DeviceIdType.MESH


def far_first(count):
    return sorted(range(1, count), key=lambda step: -min(step, count - step))


def kernel(
    ny, nz,
    features_hbm, scale_hbm, weight_hbm, bias_hbm, rows_hbm, cols_hbm, masks_hbm, cotangent_hbm,
    hidden_ref, grad_features_ref, grad_weight_ref, grad_bias_ref,
    features_ref, scale_ref, weight_ref, bias_ref, row_ids, col_ids, masks_ref, cotangent_ref,
    message_ids, earlier, last, owners,
    masks, masks_t, gathered, products, pair_out, pair_in, edge_out, edge_in, ring_out, ring_in,
    messages, back, back_edge_out, back_edge_in, back_out, back_in,
    parts, parts_in, halves, y_in, x_terms, z_terms, finals,
    load_sems, send_sems, recv_sems,
):
    f32, bf16 = jnp.float32, jnp.bfloat16
    slots = masks.shape[0]
    row, col = lax.axis_index("row"), lax.axis_index("col")
    xl, y = row // ny, row % ny
    xh, z, core = col // (2 * nz), (col % (2 * nz)) // 2, col % 2

    def row_of(x_lo, y_at):
        return x_lo * ny + y_at

    def col_of(x_hi, z_at, core_at):
        return x_hi * (2 * nz) + z_at * 2 + core_at

    sibling = (row, col_of(xh, z, 1 - core))
    lo_partner = (row_of(1 - xl, y), col)
    hi_partner = (row, col_of(1 - xh, z, core))
    far_partner = (row_of(1 - xl, y), col_of(1 - xh, z, core))
    y_far, z_far = far_first(ny), far_first(nz)
    y_peer = {j: (row_of(xl, (y + j) % ny), col) for j in y_far}
    z_peer = {j: (row, col_of(xh, (z + j) % nz, core)) for j in z_far}

    barrier = pltpu.get_barrier_semaphore()
    everyone = [sibling, lo_partner, hi_partner, far_partner]
    everyone = [y_peer[j] for j in y_far] + everyone + [z_peer[j] for j in z_far]
    for peer in everyone:
        pl.semaphore_signal(barrier, inc=1, device_id=peer, device_id_type=MESH)

    loads = []
    for number, (src, dst) in enumerate((
        (features_hbm, features_ref), (scale_hbm, scale_ref), (rows_hbm, row_ids),
        (cols_hbm, col_ids), (masks_hbm, masks_ref), (weight_hbm, weight_ref),
        (bias_hbm, bias_ref), (cotangent_hbm, cotangent_ref),
    )):
        load = pltpu.make_async_copy(src, dst, load_sems.at[number])
        load.start()
        loads.append(load)

    started = []

    def send(src, dst, peer):
        number = len(started)
        copy = pltpu.make_async_remote_copy(
            src_ref=src, dst_ref=dst, send_sem=send_sems.at[number], recv_sem=recv_sems.at[number],
            device_id=peer, device_id_type=MESH,
        )
        started.append(copy)
        copy.start()
        return copy

    loads[0].wait()
    loads[1].wait()
    scale = jnp.broadcast_to(scale_ref[...].astype(f32), (128, 128)).T
    gathered[row] = (scale * features_ref[...].astype(f32)).astype(bf16)
    pl.semaphore_wait(barrier, len(everyone))

    own = gathered.at[row]
    direct = {j: send(own, own, y_peer[j]) for j in y_far}
    swapped = [send(own, own, lo_partner)]

    for load in loads[2:5]:
        load.wait()
    def find_owner(place, carry):
        found = slots
        for slot in range(slots):
            found = jnp.where(row_ids[0, 0, slot] == place, slot, found)
        owners[place] = found
        return carry

    def prepare(slot, carry):
        masks[slot] = masks_ref[0, 0, slot].astype(f32).astype(bf16)
        return carry

    lax.fori_loop(0, slots, prepare, 0)
    products[slots] = jnp.zeros((128, 128), f32)

    for j in y_far:
        direct[j].wait_recv()
        block = gathered.at[row_of(xl, (y - j) % ny)]
        swapped.append(send(block, block, lo_partner))
    lax.fori_loop(0, 4 * nz, find_owner, 0)
    for copy in swapped:
        copy.wait_recv()

    for slot in range(slots):
        products[slot] = jnp.dot(
            masks[slot], gathered[col_ids[0, 0, slot]], preferred_element_type=f32
        )

    def term(x_hi, j, core_at):
        return products[owners[col_of(x_hi, (z + j) % nz, core_at)]]

    z_order = z_far + [0]
    group = 3
    pair_copies = {}
    for piece, x_hi in enumerate((1 - xh, xh)):
        for place, j in enumerate(z_order):
            pair_out[piece, place] = term(x_hi, j, 1 - core).astype(bf16)
            if place % group == group - 1:
                span = pl.ds(place - group + 1, group)
                pair_copies[piece, place // group] = send(
                    pair_out.at[piece, span], pair_in.at[piece, span], sibling
                )
    edges = {}
    for place, j in enumerate(z_order):
        if place % group == 0:
            pair_copies[0, place // group].wait_recv()
        total = term(1 - xh, j, core) + pair_in[0, place].astype(f32)
        edge_out[place] = total.astype(bf16)
        edges[j] = send(edge_out.at[place], edge_in.at[place], hi_partner)
    direct = {}
    summed = None
    for place, j in enumerate(z_order):
        if place % group == 0:
            pair_copies[1, place // group].wait_recv()
        total = term(xh, j, core) + pair_in[1, place].astype(f32)
        edges[j].wait_recv()
        total = total + edge_in[place].astype(f32)
        if j == 0:
            summed = total
        else:
            ring_out[j - 1] = total.astype(bf16)
            direct[j] = send(ring_out.at[j - 1], ring_in.at[j - 1], z_peer[j])
    for slot in range(slots):
        row_id = row_ids[0, 0, slot]
        message_ids[slot] = (
            (row_id % 2) * (2 * nz) + (row_id // (2 * nz)) * nz + (row_id % (2 * nz)) // 2
        )
        found = slots
        for other in range(slot):
            found = jnp.where(col_ids[0, 0, other] == col_ids[0, 0, slot], other, found)
        earlier[slot] = found

    def find_last(place, carry):
        found = slots
        for slot in range(slots):
            found = jnp.where(col_ids[0, 0, slot] == place, slot, found)
        last[place] = found
        return carry

    def transpose(slot, carry):
        masks_t[slot] = masks_ref[0, 0, slot].astype(f32).T.astype(bf16)
        return carry

    lax.fori_loop(0, 2 * ny, find_last, 0)
    lax.fori_loop(0, slots, transpose, 0)
    back[slots] = jnp.zeros((128, 128), f32)
    for load in loads[5:]:
        load.wait()
    for j in z_far:
        direct[j].wait_recv()
        summed = summed + ring_in[j - 1].astype(f32)

    aggregated = (scale * summed).astype(bf16)
    weight = weight_ref[...]
    preact = jnp.dot(aggregated, weight, preferred_element_type=f32) + bias_ref[...]
    root = math.sqrt(2.0 / math.pi)
    square = preact * preact
    slope = jnp.tanh(root * (preact + 0.044715 * (square * preact)))
    cdf = 0.5 * (1.0 + slope)
    derivative = cdf + preact * (0.5 * (1.0 - slope * slope) * (root * (1.0 + 0.134145 * square)))
    grad_pre = (cotangent_ref[...].astype(f32) * derivative).astype(bf16)
    message = scale * lax.dot_general(
        grad_pre, weight, (((1,), (1,)), ((), ())), preferred_element_type=f32
    )

    shared = []

    def message_at(x_hi, z_at):
        return messages.at[(core * 2 + x_hi) * nz + z_at]

    def share(block):
        shared.append(send(block, block, sibling))

    messages[(core * 2 + xh) * nz + z] = message.astype(bf16)
    own = message_at(xh, z)
    direct = {j: send(own, own, z_peer[j]) for j in z_far}
    swapped = [send(own, own, hi_partner)]
    share(own)

    chunk = parts.shape[2]

    hidden_ref[...] = (preact * cdf).astype(bf16)
    weight_part = lax.dot_general(
        aggregated, grad_pre, (((0,), (0,)), ((), ())), preferred_element_type=f32
    )
    bias_part = jnp.sum(grad_pre.astype(f32), axis=0, keepdims=True)
    lines = lax.broadcasted_iota(jnp.int32, (chunk, 128), 0)
    bias_tile = jnp.where(
        lines == 0, bias_part[:, :128], jnp.where(lines == 1, bias_part[:, 128:], 0.0)
    )
    for core_at in (0, 1):
        for y_at in range(ny):
            first = (core_at * ny + y_at) * chunk
            parts[core_at, y_at, :, :256] = weight_part[first : first + chunk]
            parts[core_at, y_at, :, 256:] = bias_tile
    pair = send(parts.at[1 - core], parts_in, sibling)
    pair.wait_recv()
    halves[...] = parts[core] + parts_in[...]
    y_copies = {j: send(halves.at[(y + j) % ny], y_in.at[j - 1], y_peer[j]) for j in y_far}

    for number, j in enumerate(z_far):
        direct[j].wait_recv()
        block = message_at(xh, (z - j) % nz)
        swapped.append(send(block, block, hi_partner))
        share(block)
        if number == nz // 2:
            total = halves[y]
            for j in y_far:
                y_copies[j].wait_recv()
                total = total + y_in[j - 1]
            x_at = xh * 2 + xl
            x_terms[x_at] = total
            x_copies = [
                send(x_terms.at[x_at], x_terms.at[x_at], peer)
                for peer in (lo_partner, hi_partner, far_partner)
            ]

    for copy in x_copies:
        copy.wait_recv()
    z_terms[z] = (x_terms[0] + x_terms[1]) + (x_terms[2] + x_terms[3])
    z_copies = [send(z_terms.at[z], z_terms.at[z], z_peer[j]) for j in z_far]


    for place, copy in enumerate(swapped):
        copy.wait_recv()
        share(message_at(1 - xh, z if place == 0 else (z - z_far[place - 1]) % nz))

    for copy in shared:
        copy.wait_recv()

    for slot in range(slots):
        product = jnp.dot(
            masks_t[slot], messages[message_ids[slot]], preferred_element_type=f32
        )
        back[slot] = product + back[earlier[slot]]

    def back_term(x_lo, j):
        return back[last[row_of(x_lo, (y + j) % ny)]]

    y_order = y_far + [0]
    edges = {}
    for place, j in enumerate(y_order):
        back_edge_out[place] = back_term(1 - xl, j).astype(bf16)
        edges[j] = send(back_edge_out.at[place], back_edge_in.at[place], lo_partner)
    direct = {}
    summed = None
    for place, j in enumerate(y_order):
        total = back_term(xl, j)
        edges[j].wait_recv()
        total = total + back_edge_in[place].astype(f32)
        if j == 0:
            summed = total
        else:
            back_out[j - 1] = total.astype(bf16)
            direct[j] = send(back_out.at[j - 1], back_in.at[j - 1], y_peer[j])

    for copy in z_copies:
        copy.wait_recv()
    total = z_terms[0]
    for z_at in range(1, nz):
        total = total + z_terms[z_at]
    finals[core, y] = total
    own = finals.at[core, y]
    y_copies = [send(own, own, y_peer[j]) for j in y_far]

    for j in y_far:
        direct[j].wait_recv()
        summed = summed + back_in[j - 1].astype(f32)
    grad_features_ref[...] = (scale * summed).astype(bf16)

    for copy in y_copies:
        copy.wait_recv()
    pair = send(finals.at[core], finals.at[core], sibling)
    for copy in started[:-1]:
        copy.wait_send()
    pair.wait()
    for core_at in (0, 1):
        for y_at in range(ny):
            first = (core_at * ny + y_at) * chunk
            grad_weight_ref[first : first + chunk, :] = finals[core_at, y_at, :, :256]
    grad_bias_ref[...] = finals[0, 0, 0:2, 256:]


def store(*refs):
    for number in range(4):
        refs[4 + number][...] = refs[number][...]


def copies_of(ny, nz):
    forward = (2 * ny - 1) + 2 * (nz // 3) + nz + (nz - 1)
    backward = (2 * nz - 1) + 2 * nz + ny + (ny - 1)
    weights = 1 + (ny - 1) + 3 + (nz - 1) + (ny - 1) + 1
    return forward + backward + weights


def on_device(features, node_scale, weight, bias, block_rows, block_cols, block_masks, out_grad):
    ny, nz = lax.axis_size("row") // 2, lax.axis_size("col") // 4
    slots = block_masks.shape[2]
    bf16, f32, i32 = jnp.bfloat16, jnp.float32, jnp.int32
    chunk = weight.shape[0] // (2 * ny)
    block = (128, 128)
    anywhere = pl.BlockSpec(memory_space=pl.ANY)
    vmem = pl.BlockSpec(memory_space=pltpu.VMEM)
    copies = copies_of(ny, nz)
    results = (
        jax.ShapeDtypeStruct((128, 256), bf16),
        jax.ShapeDtypeStruct(block, bf16),
        jax.ShapeDtypeStruct((128, 256), f32),
        jax.ShapeDtypeStruct((2, 128), f32),
    )
    outs = pl.pallas_call(
        functools.partial(kernel, ny, nz),
        out_shape=results,
        in_specs=[anywhere] * 8,
        out_specs=(vmem,) * 4,
        scratch_shapes=[
            pltpu.VMEM(block, bf16),
            pltpu.VMEM((1, 128), bf16),
            pltpu.VMEM((128, 256), bf16),
            pltpu.VMEM((1, 256), f32),
            pltpu.SMEM((1, 1, slots), i32),
            pltpu.SMEM((1, 1, slots), i32),
            pltpu.VMEM((1, 1, slots) + block, i32),
            pltpu.VMEM((128, 256), bf16),
            pltpu.SMEM((slots,), i32),
            pltpu.SMEM((slots,), i32),
            pltpu.SMEM((2 * ny,), i32),
            pltpu.SMEM((4 * nz,), i32),
            pltpu.VMEM((slots,) + block, bf16),
            pltpu.VMEM((slots,) + block, bf16),
            pltpu.VMEM((2 * ny,) + block, bf16),
            pltpu.VMEM((slots + 1,) + block, f32),
            pltpu.VMEM((2, nz) + block, bf16),
            pltpu.VMEM((2, nz) + block, bf16),
            pltpu.VMEM((nz,) + block, bf16),
            pltpu.VMEM((nz,) + block, bf16),
            pltpu.VMEM((nz - 1,) + block, bf16),
            pltpu.VMEM((nz - 1,) + block, bf16),
            pltpu.VMEM((4 * nz,) + block, bf16),
            pltpu.VMEM((slots + 1,) + block, f32),
            pltpu.VMEM((ny,) + block, bf16),
            pltpu.VMEM((ny,) + block, bf16),
            pltpu.VMEM((ny - 1,) + block, bf16),
            pltpu.VMEM((ny - 1,) + block, bf16),
            pltpu.VMEM((2, ny, chunk, 384), f32),
            pltpu.VMEM((ny, chunk, 384), f32),
            pltpu.VMEM((ny, chunk, 384), f32),
            pltpu.VMEM((ny - 1, chunk, 384), f32),
            pltpu.VMEM((4, chunk, 384), f32),
            pltpu.VMEM((nz, chunk, 384), f32),
            pltpu.VMEM((2, ny, chunk, 384), f32),
            pltpu.SemaphoreType.DMA((8,)),
            pltpu.SemaphoreType.DMA((copies,)),
            pltpu.SemaphoreType.DMA((copies,)),
        ],
        compiler_params=pltpu.CompilerParams(
            collective_id=0, has_side_effects=True, vmem_limit_bytes=60 * 1024 * 1024
        ),
        cost_estimate=pl.CostEstimate(
            flops=200_000_000, bytes_accessed=2_000_000, transcendentals=32768
        ),
    )(
        features, node_scale.reshape(1, 128), weight, bias.reshape(1, 256),
        block_rows, block_cols, block_masks, out_grad,
    )
    hidden, grad_features, grad_weight, grad_bias = pl.pallas_call(
        store,
        out_shape=results,
        in_specs=[vmem] * 4,
        out_specs=(vmem,) * 4,
    )(*outs)
    return hidden, grad_features, grad_weight, grad_bias.reshape(256)


def solution(mesh):
    return jax.shard_map(
        on_device,
        mesh=mesh,
        in_specs=(
            P(("row", "col"), None),
            P(("row", "col")),
            P(),
            P(),
            P("row", "col", None),
            P("row", "col", None),
            P("row", "col", None, None, None),
            P(("row", "col"), None),
        ),
        out_specs=(P(("row", "col"), None), P(("row", "col"), None), P(), P()),
        check_vma=False,
    )
```

```python
import functools
import math

import jax
import jax.numpy as jnp
from jax import lax
from jax.experimental import pallas as pl
from jax.experimental.pallas import tpu as pltpu
from jax.sharding import PartitionSpec as P

MESH = pl.DeviceIdType.MESH


def far_first(count):
    return sorted(range(1, count), key=lambda step: -min(step, count - step))


def kernel(
    ny, nz,
    features_hbm, scale_hbm, weight_hbm, bias_hbm, rows_hbm, cols_hbm, masks_hbm, cotangent_hbm,
    hidden_ref, grad_features_ref, grad_weight_ref, grad_bias_ref,
    features_ref, scale_ref, weight_ref, bias_ref, row_ids, col_ids, masks_ref, cotangent_ref,
    message_ids, earlier, last, owners,
    masks, masks_t, gathered, products, pair_out, pair_in, edge_out, edge_in, ring_out, ring_in,
    messages, back, back_edge_out, back_edge_in, back_out, back_in,
    parts, parts_in, halves, y_in, x_terms, z_terms, finals,
    load_sems, send_sems, recv_sems,
):
    f32, bf16 = jnp.float32, jnp.bfloat16
    slots = masks.shape[0]
    row, col = lax.axis_index("row"), lax.axis_index("col")
    xl, y = row // ny, row % ny
    xh, z, core = col // (2 * nz), (col % (2 * nz)) // 2, col % 2

    def row_of(x_lo, y_at):
        return x_lo * ny + y_at

    def col_of(x_hi, z_at, core_at):
        return x_hi * (2 * nz) + z_at * 2 + core_at

    sibling = (row, col_of(xh, z, 1 - core))
    lo_partner = (row_of(1 - xl, y), col)
    hi_partner = (row, col_of(1 - xh, z, core))
    far_partner = (row_of(1 - xl, y), col_of(1 - xh, z, core))
    y_far, z_far = far_first(ny), far_first(nz)
    y_peer = {j: (row_of(xl, (y + j) % ny), col) for j in y_far}
    z_peer = {j: (row, col_of(xh, (z + j) % nz, core)) for j in z_far}

    barrier = pltpu.get_barrier_semaphore()
    everyone = [sibling, lo_partner, hi_partner, far_partner]
    everyone = [y_peer[j] for j in y_far] + everyone + [z_peer[j] for j in z_far]
    for peer in everyone:
        pl.semaphore_signal(barrier, inc=1, device_id=peer, device_id_type=MESH)

    loads = []
    for number, (src, dst) in enumerate((
        (features_hbm, features_ref), (scale_hbm, scale_ref), (rows_hbm, row_ids),
        (cols_hbm, col_ids), (masks_hbm, masks_ref), (weight_hbm, weight_ref),
        (bias_hbm, bias_ref), (cotangent_hbm, cotangent_ref),
    )):
        load = pltpu.make_async_copy(src, dst, load_sems.at[number])
        load.start()
        loads.append(load)

    started = []

    def send(src, dst, peer):
        number = len(started)
        copy = pltpu.make_async_remote_copy(
            src_ref=src, dst_ref=dst, send_sem=send_sems.at[number], recv_sem=recv_sems.at[number],
            device_id=peer, device_id_type=MESH,
        )
        started.append(copy)
        copy.start()
        return copy

    loads[0].wait()
    loads[1].wait()
    scale = jnp.broadcast_to(scale_ref[...].astype(f32), (128, 128)).T
    gathered[row] = (scale * features_ref[...].astype(f32)).astype(bf16)
    pl.semaphore_wait(barrier, len(everyone))

    own = gathered.at[row]
    direct = {j: send(own, own, y_peer[j]) for j in y_far}
    swapped = [send(own, own, lo_partner)]

    for load in loads[2:5]:
        load.wait()
    def find_owner(place, carry):
        found = slots
        for slot in range(slots):
            found = jnp.where(row_ids[0, 0, slot] == place, slot, found)
        owners[place] = found
        return carry

    def prepare(slot, carry):
        masks[slot] = masks_ref[0, 0, slot].astype(f32).astype(bf16)
        return carry

    lax.fori_loop(0, slots, prepare, 0)
    products[slots] = jnp.zeros((128, 128), f32)

    for j in y_far:
        direct[j].wait_recv()
        block = gathered.at[row_of(xl, (y - j) % ny)]
        swapped.append(send(block, block, lo_partner))
    lax.fori_loop(0, 4 * nz, find_owner, 0)
    for copy in swapped:
        copy.wait_recv()

    for slot in range(slots):
        products[slot] = jnp.dot(
            masks[slot], gathered[col_ids[0, 0, slot]], preferred_element_type=f32
        )

    def term(x_hi, j, core_at):
        return products[owners[col_of(x_hi, (z + j) % nz, core_at)]]

    z_order = z_far + [0]
    group = 3
    pair_copies = {}
    for piece, x_hi in enumerate((1 - xh, xh)):
        for place, j in enumerate(z_order):
            pair_out[piece, place] = term(x_hi, j, 1 - core).astype(bf16)
            if place % group == group - 1:
                span = pl.ds(place - group + 1, group)
                pair_copies[piece, place // group] = send(
                    pair_out.at[piece, span], pair_in.at[piece, span], sibling
                )
    edges = {}
    for place, j in enumerate(z_order):
        if place % group == 0:
            pair_copies[0, place // group].wait_recv()
        total = term(1 - xh, j, core) + pair_in[0, place].astype(f32)
        edge_out[place] = total.astype(bf16)
        edges[j] = send(edge_out.at[place], edge_in.at[place], hi_partner)
    reach = nz // 4
    half = pl.ds(0, 64), pl.ds(64, 64)

    def near_sum(j):
        place = z_order.index(j)
        if place // group not in taken:
            taken.add(place // group)
            pair_copies[1, place // group].wait_recv()
        total = term(xh, j, core) + pair_in[1, place].astype(f32)
        edges[j].wait_recv()
        return total + edge_in[place].astype(f32)

    taken = set()
    direct, relayed = {}, {}
    far_steps = [j for j in z_far if reach < j < nz - reach]
    near_steps = [j for j in z_far if j not in far_steps and j not in (reach, nz - reach)]
    for j in far_steps:
        ring_out[j - 1] = near_sum(j).astype(bf16)
        if 2 * j == nz:
            for way, hop in enumerate((reach, nz - reach)):
                relayed[j, way] = send(
                    ring_out.at[j - 1, half[way]], ring_in.at[j - 1, half[way]], z_peer[hop]
                )
        else:
            hop = j - reach if 2 * j < nz else j + reach
            relayed[j] = send(ring_out.at[j - 1], ring_in.at[j - 1], z_peer[hop])
    relay_sums = {j: near_sum(j) for j in (reach, nz - reach)}
    for j in near_steps:
        ring_out[j - 1] = near_sum(j).astype(bf16)
        direct[j] = send(ring_out.at[j - 1], ring_in.at[j - 1], z_peer[j])
    summed = near_sum(0)
    for way, j in enumerate((reach, nz - reach)):
        total = relay_sums[j]
        for far in far_steps:
            if 2 * far != nz and (2 * far < nz) == (way == 0):
                relayed[far].wait_recv()
                total = total + ring_in[far - 1].astype(f32)
        relayed[nz // 2, way].wait_recv()
        middle = ring_in[nz // 2 - 1, 64 * way : 64 * way + 64, :].astype(f32)
        if way == 0:
            ring_out[j - 1, :64, :] = (total[:64] + middle).astype(bf16)
            ring_out[j - 1, 64:, :] = total[64:].astype(bf16)
        else:
            ring_out[j - 1, :64, :] = total[:64].astype(bf16)
            ring_out[j - 1, 64:, :] = (total[64:] + middle).astype(bf16)
        direct[j] = send(ring_out.at[j - 1], ring_in.at[j - 1], z_peer[j])

    for slot in range(slots):
        row_id = row_ids[0, 0, slot]
        message_ids[slot] = (
            (row_id % 2) * (2 * nz) + (row_id // (2 * nz)) * nz + (row_id % (2 * nz)) // 2
        )
        found = slots
        for other in range(slot):
            found = jnp.where(col_ids[0, 0, other] == col_ids[0, 0, slot], other, found)
        earlier[slot] = found

    def find_last(place, carry):
        found = slots
        for slot in range(slots):
            found = jnp.where(col_ids[0, 0, slot] == place, slot, found)
        last[place] = found
        return carry

    def transpose(slot, carry):
        masks_t[slot] = masks_ref[0, 0, slot].astype(f32).T.astype(bf16)
        return carry

    lax.fori_loop(0, 2 * ny, find_last, 0)
    lax.fori_loop(0, slots, transpose, 0)
    back[slots] = jnp.zeros((128, 128), f32)
    for load in loads[5:]:
        load.wait()
    for j in near_steps + [reach, nz - reach]:
        direct[j].wait_recv()
        summed = summed + ring_in[j - 1].astype(f32)

    aggregated = (scale * summed).astype(bf16)
    weight = weight_ref[...]
    preact = jnp.dot(aggregated, weight, preferred_element_type=f32) + bias_ref[...]
    root = math.sqrt(2.0 / math.pi)
    square = preact * preact
    slope = jnp.tanh(root * (preact + 0.044715 * (square * preact)))
    cdf = 0.5 * (1.0 + slope)
    derivative = cdf + preact * (0.5 * (1.0 - slope * slope) * (root * (1.0 + 0.134145 * square)))
    grad_pre = (cotangent_ref[...].astype(f32) * derivative).astype(bf16)
    message = scale * lax.dot_general(
        grad_pre, weight, (((1,), (1,)), ((), ())), preferred_element_type=f32
    )

    shared = []

    def message_at(x_hi, z_at):
        return messages.at[(core * 2 + x_hi) * nz + z_at]

    def share(block):
        shared.append(send(block, block, sibling))

    messages[(core * 2 + xh) * nz + z] = message.astype(bf16)
    own = message_at(xh, z)
    direct = {j: send(own, own, z_peer[j]) for j in (reach, nz - reach)}
    swapped = {0: send(own, own, hi_partner)}
    for j in near_steps:
        direct[j] = send(own, own, z_peer[j])
    share(own)

    chunk = parts.shape[2]

    hidden_ref[...] = (preact * cdf).astype(bf16)
    weight_part = lax.dot_general(
        aggregated, grad_pre, (((0,), (0,)), ((), ())), preferred_element_type=f32
    )
    bias_part = jnp.sum(grad_pre.astype(f32), axis=0, keepdims=True)
    lines = lax.broadcasted_iota(jnp.int32, (chunk, 128), 0)
    bias_tile = jnp.where(
        lines == 0, bias_part[:, :128], jnp.where(lines == 1, bias_part[:, 128:], 0.0)
    )
    for core_at in (0, 1):
        for y_at in range(ny):
            first = (core_at * ny + y_at) * chunk
            parts[core_at, y_at, :, :256] = weight_part[first : first + chunk]
            parts[core_at, y_at, :, 256:] = bias_tile
    pair = send(parts.at[1 - core], parts_in, sibling)
    def pass_on(j):
        block = message_at(xh, (z - j) % nz)
        swapped[j] = send(block, block, hi_partner)
        share(block)

    relayed = {}
    for way, j in enumerate((reach, nz - reach)):
        direct[j].wait_recv()
        place = (core * 2 + xh) * nz + (z - j) % nz
        for hop in range(reach, 0, -1):
            far = reach + hop if way == 0 else nz - reach - hop
            peer = z_peer[hop if way == 0 else nz - hop]
            if hop == reach:
                part = messages.at[place, half[way]]
                relayed[far, way] = send(part, part, peer)
            else:
                part = messages.at[place]
                relayed[far] = send(part, part, peer)
        pass_on(j)
    for j in near_steps:
        direct[j].wait_recv()
        pass_on(j)

    pair.wait_recv()
    halves[...] = parts[core] + parts_in[...]
    y_copies = {j: send(halves.at[(y + j) % ny], y_in.at[j - 1], y_peer[j]) for j in y_far}

    for j in far_steps[::-1]:
        if 2 * j == nz:
            relayed[j, 0].wait_recv()
            relayed[j, 1].wait_recv()
        else:
            relayed[j].wait_recv()
        pass_on(j)

    order = [0, reach, nz - reach] + near_steps
    for j in order:
        swapped[j].wait_recv()
        share(message_at(1 - xh, (z - j) % nz))

    total = halves[y]
    for j in y_far:
        y_copies[j].wait_recv()
        total = total + y_in[j - 1]
    x_at = xh * 2 + xl
    x_terms[x_at] = total
    x_copies = [
        send(x_terms.at[x_at], x_terms.at[x_at], peer)
        for peer in (lo_partner, hi_partner, far_partner)
    ]

    for j in far_steps[::-1]:
        swapped[j].wait_recv()
        share(message_at(1 - xh, (z - j) % nz))

    for copy in x_copies:
        copy.wait_recv()
    z_terms[z] = (x_terms[0] + x_terms[1]) + (x_terms[2] + x_terms[3])
    z_copies = [send(z_terms.at[z], z_terms.at[z], z_peer[j]) for j in z_far]

    for copy in shared:
        copy.wait_recv()

    for slot in range(slots):
        product = jnp.dot(
            masks_t[slot], messages[message_ids[slot]], preferred_element_type=f32
        )
        back[slot] = product + back[earlier[slot]]

    def back_term(x_lo, j):
        return back[last[row_of(x_lo, (y + j) % ny)]]

    y_order = y_far + [0]
    edges = {}
    for place, j in enumerate(y_order):
        back_edge_out[place] = back_term(1 - xl, j).astype(bf16)
        edges[j] = send(back_edge_out.at[place], back_edge_in.at[place], lo_partner)
    direct = {}
    summed = None
    for place, j in enumerate(y_order):
        total = back_term(xl, j)
        edges[j].wait_recv()
        total = total + back_edge_in[place].astype(f32)
        if j == 0:
            summed = total
        else:
            back_out[j - 1] = total.astype(bf16)
            direct[j] = send(back_out.at[j - 1], back_in.at[j - 1], y_peer[j])

    for copy in z_copies:
        copy.wait_recv()
    total = z_terms[0]
    for z_at in range(1, nz):
        total = total + z_terms[z_at]
    finals[core, y] = total
    own = finals.at[core, y]
    y_copies = [send(own, own, y_peer[j]) for j in y_far]

    for j in y_far:
        direct[j].wait_recv()
        summed = summed + back_in[j - 1].astype(f32)
    grad_features_ref[...] = (scale * summed).astype(bf16)

    for copy in y_copies:
        copy.wait_recv()
    pair = send(finals.at[core], finals.at[core], sibling)
    for copy in started[:-1]:
        copy.wait_send()
    pair.wait()
    for core_at in (0, 1):
        for y_at in range(ny):
            first = (core_at * ny + y_at) * chunk
            grad_weight_ref[first : first + chunk, :] = finals[core_at, y_at, :, :256]
    grad_bias_ref[...] = finals[0, 0, 0:2, 256:]


def store(*refs):
    for number in range(4):
        refs[4 + number][...] = refs[number][...]


def copies_of(ny, nz):
    forward = (2 * ny - 1) + 2 * (nz // 3) + nz + nz
    backward = nz + nz + 2 * nz + ny + (ny - 1)
    weights = 1 + (ny - 1) + 3 + (nz - 1) + (ny - 1) + 1
    return forward + backward + weights


def on_device(features, node_scale, weight, bias, block_rows, block_cols, block_masks, out_grad):
    ny, nz = lax.axis_size("row") // 2, lax.axis_size("col") // 4
    slots = block_masks.shape[2]
    bf16, f32, i32 = jnp.bfloat16, jnp.float32, jnp.int32
    chunk = weight.shape[0] // (2 * ny)
    block = (128, 128)
    anywhere = pl.BlockSpec(memory_space=pl.ANY)
    vmem = pl.BlockSpec(memory_space=pltpu.VMEM)
    copies = copies_of(ny, nz)
    results = (
        jax.ShapeDtypeStruct((128, 256), bf16),
        jax.ShapeDtypeStruct(block, bf16),
        jax.ShapeDtypeStruct((128, 256), f32),
        jax.ShapeDtypeStruct((2, 128), f32),
    )
    outs = pl.pallas_call(
        functools.partial(kernel, ny, nz),
        out_shape=results,
        in_specs=[anywhere] * 8,
        out_specs=(vmem,) * 4,
        scratch_shapes=[
            pltpu.VMEM(block, bf16),
            pltpu.VMEM((1, 128), bf16),
            pltpu.VMEM((128, 256), bf16),
            pltpu.VMEM((1, 256), f32),
            pltpu.SMEM((1, 1, slots), i32),
            pltpu.SMEM((1, 1, slots), i32),
            pltpu.VMEM((1, 1, slots) + block, i32),
            pltpu.VMEM((128, 256), bf16),
            pltpu.SMEM((slots,), i32),
            pltpu.SMEM((slots,), i32),
            pltpu.SMEM((2 * ny,), i32),
            pltpu.SMEM((4 * nz,), i32),
            pltpu.VMEM((slots,) + block, bf16),
            pltpu.VMEM((slots,) + block, bf16),
            pltpu.VMEM((2 * ny,) + block, bf16),
            pltpu.VMEM((slots + 1,) + block, f32),
            pltpu.VMEM((2, nz) + block, bf16),
            pltpu.VMEM((2, nz) + block, bf16),
            pltpu.VMEM((nz,) + block, bf16),
            pltpu.VMEM((nz,) + block, bf16),
            pltpu.VMEM((nz - 1,) + block, bf16),
            pltpu.VMEM((nz - 1,) + block, bf16),
            pltpu.VMEM((4 * nz,) + block, bf16),
            pltpu.VMEM((slots + 1,) + block, f32),
            pltpu.VMEM((ny,) + block, bf16),
            pltpu.VMEM((ny,) + block, bf16),
            pltpu.VMEM((ny - 1,) + block, bf16),
            pltpu.VMEM((ny - 1,) + block, bf16),
            pltpu.VMEM((2, ny, chunk, 384), f32),
            pltpu.VMEM((ny, chunk, 384), f32),
            pltpu.VMEM((ny, chunk, 384), f32),
            pltpu.VMEM((ny - 1, chunk, 384), f32),
            pltpu.VMEM((4, chunk, 384), f32),
            pltpu.VMEM((nz, chunk, 384), f32),
            pltpu.VMEM((2, ny, chunk, 384), f32),
            pltpu.SemaphoreType.DMA((8,)),
            pltpu.SemaphoreType.DMA((copies,)),
            pltpu.SemaphoreType.DMA((copies,)),
        ],
        compiler_params=pltpu.CompilerParams(
            collective_id=0, has_side_effects=True, vmem_limit_bytes=60 * 1024 * 1024
        ),
        cost_estimate=pl.CostEstimate(
            flops=200_000_000, bytes_accessed=2_000_000, transcendentals=32768
        ),
    )(
        features, node_scale.reshape(1, 128), weight, bias.reshape(1, 256),
        block_rows, block_cols, block_masks, out_grad,
    )
    hidden, grad_features, grad_weight, grad_bias = pl.pallas_call(
        store,
        out_shape=results,
        in_specs=[vmem] * 4,
        out_specs=(vmem,) * 4,
    )(*outs)
    return hidden, grad_features, grad_weight, grad_bias.reshape(256)


def solution(mesh):
    return jax.shard_map(
        on_device,
        mesh=mesh,
        in_specs=(
            P(("row", "col"), None),
            P(("row", "col")),
            P(),
            P(),
            P("row", "col", None),
            P("row", "col", None),
            P("row", "col", None, None, None),
            P(("row", "col"), None),
        ),
        out_specs=(P(("row", "col"), None), P(("row", "col"), None), P(), P()),
        check_vma=False,
    )
```

```python
import functools
import math

import jax
import jax.numpy as jnp
from jax import lax
from jax.experimental import pallas as pl
from jax.experimental.pallas import tpu as pltpu
from jax.sharding import PartitionSpec as P

MESH = pl.DeviceIdType.MESH


def far_first(count):
    return sorted(range(1, count), key=lambda step: -min(step, count - step))


def kernel(
    ny, nz,
    features_hbm, scale_hbm, weight_hbm, bias_hbm, rows_hbm, cols_hbm, masks_hbm, cotangent_hbm,
    hidden_ref, grad_features_ref, grad_weight_ref, grad_bias_ref,
    features_ref, scale_ref, weight_ref, bias_ref, row_ids, col_ids, masks_ref, cotangent_ref,
    message_ids, earlier, last, owners,
    masks, masks_t, gathered, products, pair_out, pair_in, near_out, near_in, edge_out, edge_in, ring_out, ring_in,
    messages, back, beside_out, beside_in, back_edge_out, back_edge_in, back_out, back_in,
    parts, parts_in, halves, y_in, x_terms, z_terms, finals,
    load_sems, send_sems, recv_sems,
):
    f32, bf16 = jnp.float32, jnp.bfloat16
    slots = masks.shape[0]
    row, col = lax.axis_index("row"), lax.axis_index("col")
    xl, y = row // ny, row % ny
    xh, z, core = col // (2 * nz), (col % (2 * nz)) // 2, col % 2

    def row_of(x_lo, y_at):
        return x_lo * ny + y_at

    def col_of(x_hi, z_at, core_at):
        return x_hi * (2 * nz) + z_at * 2 + core_at

    sibling = (row, col_of(xh, z, 1 - core))
    lo_partner = (row_of(1 - xl, y), col)
    hi_partner = (row, col_of(1 - xh, z, core))
    far_partner = (row_of(1 - xl, y), col_of(1 - xh, z, core))
    y_far, z_far = far_first(ny), far_first(nz)
    y_peer = {j: (row_of(xl, (y + j) % ny), col) for j in y_far}
    reach = nz // 4
    ends = (reach, nz - reach)
    far_steps = [j for j in z_far if reach < j < nz - reach]
    near_steps = [j for j in z_far if j not in far_steps and j not in ends]
    z_peer = {
        j: (row, col_of(xh, (z + j) % nz, core)) for j in list(ends) + near_steps
    }

    barrier = pltpu.get_barrier_semaphore()
    everyone = [sibling, lo_partner, hi_partner, far_partner]
    everyone = [y_peer[j] for j in y_far] + list(z_peer.values()) + everyone
    for peer in everyone:
        pl.semaphore_signal(barrier, inc=1, device_id=peer, device_id_type=MESH)

    loads = []
    for number, (src, dst) in enumerate((
        (features_hbm, features_ref), (scale_hbm, scale_ref), (rows_hbm, row_ids),
        (cols_hbm, col_ids), (masks_hbm, masks_ref), (weight_hbm, weight_ref),
        (bias_hbm, bias_ref), (cotangent_hbm, cotangent_ref),
    )):
        load = pltpu.make_async_copy(src, dst, load_sems.at[number])
        load.start()
        loads.append(load)

    started = []

    def send(src, dst, peer):
        number = len(started)
        copy = pltpu.make_async_remote_copy(
            src_ref=src, dst_ref=dst, send_sem=send_sems.at[number], recv_sem=recv_sems.at[number],
            device_id=peer, device_id_type=MESH,
        )
        started.append(copy)
        copy.start()
        return copy

    drained = []

    def drain(count):
        for copy in started[len(drained) : count]:
            copy.wait_send()
            drained.append(copy)

    loads[0].wait()
    loads[1].wait()
    scale = jnp.broadcast_to(scale_ref[...].astype(f32), (128, 128)).T
    gathered[row] = (scale * features_ref[...].astype(f32)).astype(bf16)
    pl.semaphore_wait(barrier, len(everyone))

    own = gathered.at[row]
    direct = {j: send(own, own, y_peer[j]) for j in y_far}
    swapped = [send(own, own, lo_partner)]

    for load in loads[2:5]:
        load.wait()
    def find_owner(place, carry):
        found = slots
        for slot in range(slots):
            found = jnp.where(row_ids[0, 0, slot] == place, slot, found)
        owners[place] = found
        return carry

    def prepare(slot, carry):
        masks[slot] = masks_ref[0, 0, slot].astype(f32).astype(bf16)
        return carry

    lax.fori_loop(0, slots, prepare, 0)
    swapped[0].wait_recv()
    other = gathered.at[row_of(1 - xl, y)]
    crossed = [send(other, other, y_peer[j]) for j in (1, ny - 1)]
    products[slots] = jnp.zeros((128, 128), f32)

    for j in y_far:
        direct[j].wait_recv()
        if j not in (1, ny - 1):
            block = gathered.at[row_of(xl, (y - j) % ny)]
            swapped.append(send(block, block, lo_partner))
    lax.fori_loop(0, 4 * nz, find_owner, 0)
    for copy in swapped[1:] + crossed:
        copy.wait_recv()

    for slot in range(slots):
        products[slot] = jnp.dot(
            masks[slot], gathered[col_ids[0, 0, slot]], preferred_element_type=f32
        )

    def term(x_hi, j, core_at):
        return products[owners[col_of(x_hi, (z + j) % nz, core_at)]]

    z_order = z_far + [0]
    group = 3
    pair_copies = {}
    for piece, x_hi in enumerate((1 - xh, xh)):
        for place, j in enumerate(z_order):
            pair_out[piece, place] = term(x_hi, j, 1 - core).astype(bf16)
            if place % group == group - 1:
                span = pl.ds(place - group + 1, group)
                pair_copies[piece, place // group] = send(
                    pair_out.at[piece, span], pair_in.at[piece, span], sibling
                )
    taken = set()

    def pair_sum(piece, j):
        place = z_order.index(j)
        if (piece, place // group) not in taken:
            taken.add((piece, place // group))
            pair_copies[piece, place // group].wait_recv()
        x_hi = 1 - xh if piece == 0 else xh
        return term(x_hi, j, core) + pair_in[piece, place].astype(f32)

    edges = {}
    for place, j in enumerate(far_steps + list(ends)):
        edge_out[place] = pair_sum(0, j).astype(bf16)
        edges[j] = send(edge_out.at[place], edge_in.at[place], hi_partner)
    direct, relayed = {}, {}
    for number, j in enumerate(near_steps):
        near_out[number, 0] = pair_sum(0, j).astype(bf16)
        near_out[number, 1] = pair_sum(1, j).astype(bf16)
        direct[j] = send(near_out.at[number], near_in.at[number], z_peer[j])
    half = pl.ds(0, 64), pl.ds(64, 64)

    def far_sum(j):
        total = pair_sum(1, j)
        edges[j].wait_recv()
        return total + edge_in[(far_steps + list(ends)).index(j)].astype(f32)

    for j in far_steps:
        ring_out[j - 1] = far_sum(j).astype(bf16)
        if 2 * j == nz:
            for way, hop in enumerate(ends):
                relayed[j, way] = send(
                    ring_out.at[j - 1, half[way]], ring_in.at[j - 1, half[way]], z_peer[hop]
                )
        else:
            hop = j - reach if 2 * j < nz else j + reach
            relayed[j] = send(ring_out.at[j - 1], ring_in.at[j - 1], z_peer[hop])
    relay_sums = {j: far_sum(j) for j in ends}
    other, summed = pair_sum(0, 0), pair_sum(1, 0)
    for number, j in enumerate(near_steps):
        direct[j].wait_recv()
        other = other + near_in[number, 0].astype(f32)
        summed = summed + near_in[number, 1].astype(f32)
    edge_out[nz - 1] = other.astype(bf16)
    edges[0] = send(edge_out.at[nz - 1], edge_in.at[nz - 1], hi_partner)
    for way, j in enumerate(ends):
        total = relay_sums[j]
        for far in far_steps:
            if 2 * far != nz and (2 * far < nz) == (way == 0):
                relayed[far].wait_recv()
                total = total + ring_in[far - 1].astype(f32)
        relayed[nz // 2, way].wait_recv()
        middle = ring_in[nz // 2 - 1, 64 * way : 64 * way + 64, :].astype(f32)
        if way == 0:
            ring_out[j - 1, :64, :] = (total[:64] + middle).astype(bf16)
            ring_out[j - 1, 64:, :] = total[64:].astype(bf16)
        else:
            ring_out[j - 1, :64, :] = total[:64].astype(bf16)
            ring_out[j - 1, 64:, :] = (total[64:] + middle).astype(bf16)
        direct[j] = send(ring_out.at[j - 1], ring_in.at[j - 1], z_peer[j])

    for slot in range(slots):
        row_id = row_ids[0, 0, slot]
        message_ids[slot] = (
            (row_id % 2) * (2 * nz) + (row_id // (2 * nz)) * nz + (row_id % (2 * nz)) // 2
        )
        found = slots
        for other in range(slot):
            found = jnp.where(col_ids[0, 0, other] == col_ids[0, 0, slot], other, found)
        earlier[slot] = found

    def find_last(place, carry):
        found = slots
        for slot in range(slots):
            found = jnp.where(col_ids[0, 0, slot] == place, slot, found)
        last[place] = found
        return carry

    def transpose(slot, carry):
        masks_t[slot] = masks_ref[0, 0, slot].astype(f32).T.astype(bf16)
        return carry

    lax.fori_loop(0, 2 * ny, find_last, 0)
    lax.fori_loop(0, slots, transpose, 0)
    back[slots] = jnp.zeros((128, 128), f32)
    for load in loads[5:]:
        load.wait()
    edges[0].wait_recv()
    summed = summed + edge_in[nz - 1].astype(f32)
    for j in ends:
        direct[j].wait_recv()
        summed = summed + ring_in[j - 1].astype(f32)

    aggregated = (scale * summed).astype(bf16)
    weight = weight_ref[...]
    preact = jnp.dot(aggregated, weight, preferred_element_type=f32) + bias_ref[...]
    root = math.sqrt(2.0 / math.pi)
    square = preact * preact
    slope = jnp.tanh(root * (preact + 0.044715 * (square * preact)))
    cdf = 0.5 * (1.0 + slope)
    derivative = cdf + preact * (0.5 * (1.0 - slope * slope) * (root * (1.0 + 0.134145 * square)))
    grad_pre = (cotangent_ref[...].astype(f32) * derivative).astype(bf16)
    message = scale * lax.dot_general(
        grad_pre, weight, (((1,), (1,)), ((), ())), preferred_element_type=f32
    )

    before_messages = len(started)
    shared = []

    def message_at(x_hi, z_at):
        return messages.at[(core * 2 + x_hi) * nz + z_at]

    def share(block):
        shared.append(send(block, block, sibling))

    messages[(core * 2 + xh) * nz + z] = message.astype(bf16)
    own = message_at(xh, z)
    direct = {j: send(own, own, z_peer[j]) for j in ends}
    swapped = {0: send(own, own, hi_partner)}
    for j in near_steps:
        direct[j] = send(own, own, z_peer[j])
    share(own)

    chunk = parts.shape[2]

    hidden_ref[...] = (preact * cdf).astype(bf16)
    weight_part = lax.dot_general(
        aggregated, grad_pre, (((0,), (0,)), ((), ())), preferred_element_type=f32
    )
    bias_part = jnp.sum(grad_pre.astype(f32), axis=0, keepdims=True)
    lines = lax.broadcasted_iota(jnp.int32, (chunk, 128), 0)
    bias_tile = jnp.where(
        lines == 0, bias_part[:, :128], jnp.where(lines == 1, bias_part[:, 128:], 0.0)
    )
    for core_at in (0, 1):
        for y_at in range(ny):
            first = (core_at * ny + y_at) * chunk
            parts[core_at, y_at, :, :256] = weight_part[first : first + chunk]
            parts[core_at, y_at, :, 256:] = bias_tile
    pair = send(parts.at[1 - core], parts_in, sibling)
    drain(before_messages)
    def pass_on(j):
        block = message_at(xh, (z - j) % nz)
        swapped[j] = send(block, block, hi_partner)
        share(block)

    relayed = {}
    for way, j in enumerate(ends):
        direct[j].wait_recv()
        place = (core * 2 + xh) * nz + (z - j) % nz
        for hop in range(reach, 0, -1):
            far = reach + hop if way == 0 else nz - reach - hop
            peer = z_peer[hop if way == 0 else nz - hop]
            if hop == reach:
                part = messages.at[place, half[way]]
                relayed[far, way] = send(part, part, peer)
            else:
                part = messages.at[place]
                relayed[far] = send(part, part, peer)
        pass_on(j)
    for j in near_steps:
        direct[j].wait_recv()
        pass_on(j)

    pair.wait_recv()
    halves[...] = parts[core] + parts_in[...]
    y_copies = {j: send(halves.at[(y + j) % ny], y_in.at[j - 1], y_peer[j]) for j in y_far}

    for j in far_steps[::-1]:
        if 2 * j == nz:
            relayed[j, 0].wait_recv()
            relayed[j, 1].wait_recv()
        else:
            relayed[j].wait_recv()
        pass_on(j)

    order = [0, reach, nz - reach] + near_steps
    for j in order:
        swapped[j].wait_recv()
        share(message_at(1 - xh, (z - j) % nz))

    total = halves[y]
    for j in y_far:
        y_copies[j].wait_recv()
        total = total + y_in[j - 1]
    x_at = xh * 2 + xl
    x_terms[x_at] = total
    x_copies = [
        send(x_terms.at[x_at], x_terms.at[x_at], peer)
        for peer in (lo_partner, hi_partner, far_partner)
    ]

    for j in far_steps[::-1]:
        swapped[j].wait_recv()
        share(message_at(1 - xh, (z - j) % nz))

    for copy in x_copies:
        copy.wait_recv()
    z_terms[z] = (x_terms[0] + x_terms[1]) + (x_terms[2] + x_terms[3])
    own = z_terms.at[z]
    z_copies = {j: send(own, own, z_peer[j]) for j in list(ends) + near_steps}

    for copy in shared:
        copy.wait_recv()

    before_back = len(started)
    for slot in range(slots):
        product = jnp.dot(
            masks_t[slot], messages[message_ids[slot]], preferred_element_type=f32
        )
        back[slot] = product + back[earlier[slot]]

    def back_term(x_lo, j):
        return back[last[row_of(x_lo, (y + j) % ny)]]

    y_near = (1, ny - 1)
    y_rest = [j for j in y_far if j not in y_near]
    edges, direct = {}, {}
    for place, j in enumerate(y_rest):
        back_edge_out[place] = back_term(1 - xl, j).astype(bf16)
        edges[j] = send(back_edge_out.at[place], back_edge_in.at[place], lo_partner)
    for number, j in enumerate(y_near):
        beside_out[number, 0] = back_term(1 - xl, j).astype(bf16)
        beside_out[number, 1] = back_term(xl, j).astype(bf16)
        direct[j] = send(beside_out.at[number], beside_in.at[number], y_peer[j])
    for way, j in enumerate(ends):
        z_copies[j].wait_recv()
        block = z_terms.at[(z - j) % nz]
        for hop in range(reach - way, 0, -1):
            far = reach + hop if way == 0 else nz - reach - hop
            z_copies[far] = send(block, block, z_peer[hop if way == 0 else nz - hop])
    for place, j in enumerate(y_rest):
        total = back_term(xl, j)
        edges[j].wait_recv()
        total = total + back_edge_in[place].astype(f32)
        back_out[j - 1] = total.astype(bf16)
        direct[j] = send(back_out.at[j - 1], back_in.at[j - 1], y_peer[j])
    other, summed = back_term(1 - xl, 0), back_term(xl, 0)
    for number, j in enumerate(y_near):
        direct[j].wait_recv()
        other = other + beside_in[number, 0].astype(f32)
        summed = summed + beside_in[number, 1].astype(f32)
    back_edge_out[ny - 1] = other.astype(bf16)
    edge = send(back_edge_out.at[ny - 1], back_edge_in.at[ny - 1], lo_partner)
    drain(before_back)

    for j in near_steps + far_steps:
        z_copies[j].wait_recv()
    total = z_terms[0]
    for z_at in range(1, nz):
        total = total + z_terms[z_at]
    finals[core, y] = total
    own = finals.at[core, y]
    y_copies = [send(own, own, y_peer[j]) for j in y_far]

    edge.wait_recv()
    summed = summed + back_edge_in[ny - 1].astype(f32)
    for j in y_rest:
        direct[j].wait_recv()
        summed = summed + back_in[j - 1].astype(f32)
    grad_features_ref[...] = (scale * summed).astype(bf16)

    for copy in y_copies:
        copy.wait_recv()
    pair = send(finals.at[core], finals.at[core], sibling)
    drain(len(started))
    pair.wait_recv()
    for core_at in (0, 1):
        for y_at in range(ny):
            first = (core_at * ny + y_at) * chunk
            grad_weight_ref[first : first + chunk, :] = finals[core_at, y_at, :, :256]
    grad_bias_ref[...] = finals[0, 0, 0:2, 256:]


def store(*refs):
    for number in range(4):
        refs[4 + number][...] = refs[number][...]


def copies_of(ny, nz):
    forward = (2 * ny - 1) + 2 * (nz // 3) + (nz - 4) + nz
    backward = nz + nz + 2 * nz + (ny - 2) + (ny - 1)
    weights = 1 + (ny - 1) + 3 + (nz - 1) + (ny - 1) + 1
    return forward + backward + weights


def on_device(features, node_scale, weight, bias, block_rows, block_cols, block_masks, out_grad):
    ny, nz = lax.axis_size("row") // 2, lax.axis_size("col") // 4
    slots = block_masks.shape[2]
    bf16, f32, i32 = jnp.bfloat16, jnp.float32, jnp.int32
    chunk = weight.shape[0] // (2 * ny)
    block = (128, 128)
    anywhere = pl.BlockSpec(memory_space=pl.ANY)
    vmem = pl.BlockSpec(memory_space=pltpu.VMEM)
    copies = copies_of(ny, nz)
    results = (
        jax.ShapeDtypeStruct((128, 256), bf16),
        jax.ShapeDtypeStruct(block, bf16),
        jax.ShapeDtypeStruct((128, 256), f32),
        jax.ShapeDtypeStruct((2, 128), f32),
    )
    outs = pl.pallas_call(
        functools.partial(kernel, ny, nz),
        out_shape=results,
        in_specs=[anywhere] * 8,
        out_specs=(vmem,) * 4,
        scratch_shapes=[
            pltpu.VMEM(block, bf16),
            pltpu.VMEM((1, 128), bf16),
            pltpu.VMEM((128, 256), bf16),
            pltpu.VMEM((1, 256), f32),
            pltpu.SMEM((1, 1, slots), i32),
            pltpu.SMEM((1, 1, slots), i32),
            pltpu.VMEM((1, 1, slots) + block, i32),
            pltpu.VMEM((128, 256), bf16),
            pltpu.SMEM((slots,), i32),
            pltpu.SMEM((slots,), i32),
            pltpu.SMEM((2 * ny,), i32),
            pltpu.SMEM((4 * nz,), i32),
            pltpu.VMEM((slots,) + block, bf16),
            pltpu.VMEM((slots,) + block, bf16),
            pltpu.VMEM((2 * ny,) + block, bf16),
            pltpu.VMEM((slots + 1,) + block, f32),
            pltpu.VMEM((2, nz) + block, bf16),
            pltpu.VMEM((2, nz) + block, bf16),
            pltpu.VMEM((4, 2) + block, bf16),
            pltpu.VMEM((4, 2) + block, bf16),
            pltpu.VMEM((nz,) + block, bf16),
            pltpu.VMEM((nz,) + block, bf16),
            pltpu.VMEM((nz - 1,) + block, bf16),
            pltpu.VMEM((nz - 1,) + block, bf16),
            pltpu.VMEM((4 * nz,) + block, bf16),
            pltpu.VMEM((slots + 1,) + block, f32),
            pltpu.VMEM((2, 2) + block, bf16),
            pltpu.VMEM((2, 2) + block, bf16),
            pltpu.VMEM((ny,) + block, bf16),
            pltpu.VMEM((ny,) + block, bf16),
            pltpu.VMEM((ny - 1,) + block, bf16),
            pltpu.VMEM((ny - 1,) + block, bf16),
            pltpu.VMEM((2, ny, chunk, 384), f32),
            pltpu.VMEM((ny, chunk, 384), f32),
            pltpu.VMEM((ny, chunk, 384), f32),
            pltpu.VMEM((ny - 1, chunk, 384), f32),
            pltpu.VMEM((4, chunk, 384), f32),
            pltpu.VMEM((nz, chunk, 384), f32),
            pltpu.VMEM((2, ny, chunk, 384), f32),
            pltpu.SemaphoreType.DMA((8,)),
            pltpu.SemaphoreType.DMA((copies,)),
            pltpu.SemaphoreType.DMA((copies,)),
        ],
        compiler_params=pltpu.CompilerParams(
            collective_id=0, has_side_effects=True, vmem_limit_bytes=60 * 1024 * 1024
        ),
        cost_estimate=pl.CostEstimate(
            flops=200_000_000, bytes_accessed=2_000_000, transcendentals=32768
        ),
    )(
        features, node_scale.reshape(1, 128), weight, bias.reshape(1, 256),
        block_rows, block_cols, block_masks, out_grad,
    )
    hidden, grad_features, grad_weight, grad_bias = pl.pallas_call(
        store,
        out_shape=results,
        in_specs=[vmem] * 4,
        out_specs=(vmem,) * 4,
    )(*outs)
    return hidden, grad_features, grad_weight, grad_bias.reshape(256)


def solution(mesh):
    return jax.shard_map(
        on_device,
        mesh=mesh,
        in_specs=(
            P(("row", "col"), None),
            P(("row", "col")),
            P(),
            P(),
            P("row", "col", None),
            P("row", "col", None),
            P("row", "col", None, None, None),
            P(("row", "col"), None),
        ),
        out_specs=(P(("row", "col"), None), P(("row", "col"), None), P(), P()),
        check_vma=False,
    )
```

```python
import functools
import math

import jax
import jax.numpy as jnp
from jax import lax
from jax.experimental import pallas as pl
from jax.experimental.pallas import tpu as pltpu
from jax.sharding import PartitionSpec as P

MESH = pl.DeviceIdType.MESH


def far_first(count):
    return sorted(range(1, count), key=lambda step: -min(step, count - step))


def kernel(
    ny, nz,
    features_hbm, scale_hbm, weight_hbm, bias_hbm, rows_hbm, cols_hbm, masks_hbm, cotangent_hbm,
    hidden_ref, grad_features_ref, grad_weight_ref, grad_bias_ref,
    features_ref, scale_ref, weight_ref, bias_ref, row_ids, col_ids, masks_ref, cotangent_ref,
    message_ids, earlier, last, owners,
    masks, masks_t, gathered, products, pair_out, pair_in, near_out, near_in, edge_out, edge_in, ring_out, ring_in,
    messages, back, beside_out, beside_in, back_edge_out, back_edge_in, back_out, back_in,
    parts, parts_in, halves, y_in, x_terms, z_terms, finals,
    load_sems, send_sems, recv_sems,
):
    f32, bf16 = jnp.float32, jnp.bfloat16
    slots = masks.shape[0]
    row, col = lax.axis_index("row"), lax.axis_index("col")
    xl, y = row // ny, row % ny
    xh, z, core = col // (2 * nz), (col % (2 * nz)) // 2, col % 2

    def row_of(x_lo, y_at):
        return x_lo * ny + y_at

    def col_of(x_hi, z_at, core_at):
        return x_hi * (2 * nz) + z_at * 2 + core_at

    sibling = (row, col_of(xh, z, 1 - core))
    lo_partner = (row_of(1 - xl, y), col)
    hi_partner = (row, col_of(1 - xh, z, core))
    far_partner = (row_of(1 - xl, y), col_of(1 - xh, z, core))
    y_far, z_far = far_first(ny), far_first(nz)
    y_peer = {j: (row_of(xl, (y + j) % ny), col) for j in y_far}
    reach = nz // 4
    ends = (reach, nz - reach)
    far_steps = [j for j in z_far if reach < j < nz - reach]
    near_steps = [j for j in z_far if j not in far_steps and j not in ends]
    z_peer = {
        j: (row, col_of(xh, (z + j) % nz, core)) for j in list(ends) + near_steps
    }

    barrier = pltpu.get_barrier_semaphore()
    everyone = [sibling, lo_partner, hi_partner, far_partner]
    everyone = [y_peer[j] for j in y_far] + list(z_peer.values()) + everyone
    for peer in everyone:
        pl.semaphore_signal(barrier, inc=1, device_id=peer, device_id_type=MESH)

    loads = []
    for number, (src, dst) in enumerate((
        (features_hbm, features_ref), (scale_hbm, scale_ref), (rows_hbm, row_ids),
        (cols_hbm, col_ids), (masks_hbm, masks_ref), (weight_hbm, weight_ref),
        (bias_hbm, bias_ref), (cotangent_hbm, cotangent_ref),
    )):
        load = pltpu.make_async_copy(src, dst, load_sems.at[number])
        load.start()
        loads.append(load)

    started = []

    def send(src, dst, peer):
        number = len(started)
        copy = pltpu.make_async_remote_copy(
            src_ref=src, dst_ref=dst, send_sem=send_sems.at[number], recv_sem=recv_sems.at[number],
            device_id=peer, device_id_type=MESH,
        )
        started.append(copy)
        copy.start()
        return copy

    drained = []

    def drain(count):
        for copy in started[len(drained) : count]:
            copy.wait_send()
            drained.append(copy)

    loads[0].wait()
    loads[1].wait()
    scale = jnp.broadcast_to(scale_ref[...].astype(f32), (128, 128)).T
    gathered[row] = (scale * features_ref[...].astype(f32)).astype(bf16)
    pl.semaphore_wait(barrier, len(everyone))

    own = gathered.at[row]
    direct = {j: send(own, own, y_peer[j]) for j in y_far}
    swapped = [send(own, own, lo_partner)]

    for load in loads[2:5]:
        load.wait()
    def find_owner(place, carry):
        found = slots
        for slot in range(slots):
            found = jnp.where(row_ids[0, 0, slot] == place, slot, found)
        owners[place] = found
        return carry

    def prepare(slot, carry):
        masks[slot] = masks_ref[0, 0, slot].astype(f32).astype(bf16)
        return carry

    lax.fori_loop(0, slots, prepare, 0)
    swapped[0].wait_recv()
    other = gathered.at[row_of(1 - xl, y)]
    crossed = [send(other, other, y_peer[j]) for j in (1, ny - 1)]
    products[slots] = jnp.zeros((128, 128), f32)

    for j in y_far:
        direct[j].wait_recv()
        if j not in (1, ny - 1):
            block = gathered.at[row_of(xl, (y - j) % ny)]
            swapped.append(send(block, block, lo_partner))
    lax.fori_loop(0, 4 * nz, find_owner, 0)
    for copy in swapped[1:] + crossed:
        copy.wait_recv()

    for slot in range(slots):
        products[slot] = jnp.dot(
            masks[slot], gathered[col_ids[0, 0, slot]], preferred_element_type=f32
        )

    def term(x_hi, j, core_at):
        return products[owners[col_of(x_hi, (z + j) % nz, core_at)]]

    z_order = z_far + [0]
    group = 3
    pair_copies = {}
    for piece, x_hi in enumerate((1 - xh, xh)):
        for place, j in enumerate(z_order):
            pair_out[piece, place] = term(x_hi, j, 1 - core).astype(bf16)
            if place % group == group - 1:
                span = pl.ds(place - group + 1, group)
                pair_copies[piece, place // group] = send(
                    pair_out.at[piece, span], pair_in.at[piece, span], sibling
                )
    taken = set()

    def pair_sum(piece, j):
        place = z_order.index(j)
        if (piece, place // group) not in taken:
            taken.add((piece, place // group))
            pair_copies[piece, place // group].wait_recv()
        x_hi = 1 - xh if piece == 0 else xh
        return term(x_hi, j, core) + pair_in[piece, place].astype(f32)

    edges = {}
    for place, j in enumerate(far_steps + list(ends)):
        edge_out[place] = pair_sum(0, j).astype(bf16)
        edges[j] = send(edge_out.at[place], edge_in.at[place], hi_partner)
    direct, relayed = {}, {}
    for number, j in enumerate(near_steps):
        near_out[number, 0] = pair_sum(0, j).astype(bf16)
        near_out[number, 1] = pair_sum(1, j).astype(bf16)
        direct[j] = send(near_out.at[number], near_in.at[number], z_peer[j])
    half = pl.ds(0, 64), pl.ds(64, 64)

    def far_sum(j):
        total = pair_sum(1, j)
        edges[j].wait_recv()
        return total + edge_in[(far_steps + list(ends)).index(j)].astype(f32)

    for j in far_steps:
        ring_out[j - 1] = far_sum(j).astype(bf16)
        if 2 * j == nz:
            for way, hop in enumerate(ends):
                relayed[j, way] = send(
                    ring_out.at[j - 1, half[way]], ring_in.at[j - 1, half[way]], z_peer[hop]
                )
        else:
            hop = j - reach if 2 * j < nz else j + reach
            relayed[j] = send(ring_out.at[j - 1], ring_in.at[j - 1], z_peer[hop])
    relay_sums = {j: far_sum(j) for j in ends}
    other, summed = pair_sum(0, 0), pair_sum(1, 0)
    for number, j in enumerate(near_steps):
        direct[j].wait_recv()
        other = other + near_in[number, 0].astype(f32)
        summed = summed + near_in[number, 1].astype(f32)
    edge_out[nz - 1] = other.astype(bf16)
    edges[0] = send(edge_out.at[nz - 1], edge_in.at[nz - 1], hi_partner)
    for way, j in enumerate(ends):
        total = relay_sums[j]
        for far in far_steps:
            if 2 * far != nz and (2 * far < nz) == (way == 0):
                relayed[far].wait_recv()
                total = total + ring_in[far - 1].astype(f32)
        relayed[nz // 2, way].wait_recv()
        middle = ring_in[nz // 2 - 1, 64 * way : 64 * way + 64, :].astype(f32)
        if way == 0:
            ring_out[j - 1, :64, :] = (total[:64] + middle).astype(bf16)
            ring_out[j - 1, 64:, :] = total[64:].astype(bf16)
        else:
            ring_out[j - 1, :64, :] = total[:64].astype(bf16)
            ring_out[j - 1, 64:, :] = (total[64:] + middle).astype(bf16)
        direct[j] = send(ring_out.at[j - 1], ring_in.at[j - 1], z_peer[j])

    for slot in range(slots):
        row_id = row_ids[0, 0, slot]
        message_ids[slot] = (
            (row_id % 2) * (2 * nz) + (row_id // (2 * nz)) * nz + (row_id % (2 * nz)) // 2
        )
        found = slots
        for other in range(slot):
            found = jnp.where(col_ids[0, 0, other] == col_ids[0, 0, slot], other, found)
        earlier[slot] = found

    def find_last(place, carry):
        found = slots
        for slot in range(slots):
            found = jnp.where(col_ids[0, 0, slot] == place, slot, found)
        last[place] = found
        return carry

    def transpose(slot, carry):
        masks_t[slot] = masks_ref[0, 0, slot].astype(f32).T.astype(bf16)
        return carry

    lax.fori_loop(0, 2 * ny, find_last, 0)
    lax.fori_loop(0, slots, transpose, 0)
    back[slots] = jnp.zeros((128, 128), f32)
    for load in loads[5:]:
        load.wait()
    edges[0].wait_recv()
    summed = summed + edge_in[nz - 1].astype(f32)
    for j in ends:
        direct[j].wait_recv()
        summed = summed + ring_in[j - 1].astype(f32)

    aggregated = (scale * summed).astype(bf16)
    weight = weight_ref[...]
    preact = jnp.dot(aggregated, weight, preferred_element_type=f32) + bias_ref[...]
    root = math.sqrt(2.0 / math.pi)
    square = preact * preact
    slope = jnp.tanh(root * (preact + 0.044715 * (square * preact)))
    cdf = 0.5 * (1.0 + slope)
    derivative = cdf + preact * (0.5 * (1.0 - slope * slope) * (root * (1.0 + 0.134145 * square)))
    grad_pre = (cotangent_ref[...].astype(f32) * derivative).astype(bf16)
    message = scale * lax.dot_general(
        grad_pre, weight, (((1,), (1,)), ((), ())), preferred_element_type=f32
    )

    before_messages = len(started)
    shared = []

    def message_at(x_hi, z_at):
        return messages.at[(core * 2 + x_hi) * nz + z_at]

    def share(block):
        shared.append(send(block, block, sibling))

    messages[(core * 2 + xh) * nz + z] = message.astype(bf16)
    own = message_at(xh, z)
    direct = {j: send(own, own, z_peer[j]) for j in ends}
    swapped = {0: send(own, own, hi_partner)}
    for j in near_steps:
        direct[j] = send(own, own, z_peer[j])
    share(own)

    chunk = parts.shape[2]

    hidden_ref[...] = (preact * cdf).astype(bf16)
    weight_part = lax.dot_general(
        aggregated, grad_pre, (((0,), (0,)), ((), ())), preferred_element_type=f32
    )
    bias_part = jnp.sum(grad_pre.astype(f32), axis=0, keepdims=True)
    lines = lax.broadcasted_iota(jnp.int32, (chunk, 128), 0)
    bias_tile = jnp.where(
        lines == 0, bias_part[:, :128], jnp.where(lines == 1, bias_part[:, 128:], 0.0)
    )
    for core_at in (0, 1):
        for y_at in range(ny):
            first = (core_at * ny + y_at) * chunk
            parts[core_at, y_at, :, :256] = weight_part[first : first + chunk]
            parts[core_at, y_at, :, 256:] = bias_tile
    pair = send(parts.at[1 - core], parts_in, sibling)
    drain(before_messages)
    pair.wait_recv()
    halves[...] = parts[core] + parts_in[...]
    y_copies = {j: send(halves.at[(y + j) % ny], y_in.at[j - 1], y_peer[j]) for j in y_far}

    def pass_on(j):
        block = message_at(xh, (z - j) % nz)
        swapped[j] = send(block, block, hi_partner)
        share(block)

    relayed = {}
    for way, j in enumerate(ends):
        direct[j].wait_recv()
        place = (core * 2 + xh) * nz + (z - j) % nz
        for hop in range(reach, 0, -1):
            far = reach + hop if way == 0 else nz - reach - hop
            peer = z_peer[hop if way == 0 else nz - hop]
            if hop == reach:
                part = messages.at[place, half[way]]
                relayed[far, way] = send(part, part, peer)
            else:
                part = messages.at[place]
                relayed[far] = send(part, part, peer)
        pass_on(j)
    for j in near_steps:
        direct[j].wait_recv()
        pass_on(j)

    for number, j in enumerate(far_steps[::-1]):
        if 2 * j == nz:
            relayed[j, 0].wait_recv()
            relayed[j, 1].wait_recv()
        else:
            relayed[j].wait_recv()
        pass_on(j)
        if number == 2:
            total = halves[y]
            for j in y_far:
                y_copies[j].wait_recv()
                total = total + y_in[j - 1]
            x_at = xh * 2 + xl
            x_terms[x_at] = total
            x_copies = [
                send(x_terms.at[x_at], x_terms.at[x_at], peer)
                for peer in (lo_partner, hi_partner, far_partner)
            ]

    order = [0, reach, nz - reach] + near_steps
    for j in order:
        swapped[j].wait_recv()
        share(message_at(1 - xh, (z - j) % nz))

    for copy in x_copies:
        copy.wait_recv()
    z_terms[z] = (x_terms[0] + x_terms[1]) + (x_terms[2] + x_terms[3])
    own = z_terms.at[z]
    z_copies = {j: send(own, own, z_peer[j]) for j in list(ends) + near_steps}

    for j in far_steps[::-1]:
        swapped[j].wait_recv()
        share(message_at(1 - xh, (z - j) % nz))

    for copy in shared:
        copy.wait_recv()

    before_back = len(started)
    for slot in range(slots):
        product = jnp.dot(
            masks_t[slot], messages[message_ids[slot]], preferred_element_type=f32
        )
        back[slot] = product + back[earlier[slot]]

    def back_term(x_lo, j):
        return back[last[row_of(x_lo, (y + j) % ny)]]

    y_near = (1, ny - 1)
    y_rest = [j for j in y_far if j not in y_near]
    edges, direct = {}, {}
    for place, j in enumerate(y_rest):
        back_edge_out[place] = back_term(1 - xl, j).astype(bf16)
        edges[j] = send(back_edge_out.at[place], back_edge_in.at[place], lo_partner)
    for number, j in enumerate(y_near):
        beside_out[number, 0] = back_term(1 - xl, j).astype(bf16)
        beside_out[number, 1] = back_term(xl, j).astype(bf16)
        direct[j] = send(beside_out.at[number], beside_in.at[number], y_peer[j])
    for way, j in enumerate(ends):
        z_copies[j].wait_recv()
        block = z_terms.at[(z - j) % nz]
        for hop in range(reach - way, 0, -1):
            far = reach + hop if way == 0 else nz - reach - hop
            z_copies[far] = send(block, block, z_peer[hop if way == 0 else nz - hop])

    for place, j in enumerate(y_rest):
        total = back_term(xl, j)
        edges[j].wait_recv()
        total = total + back_edge_in[place].astype(f32)
        back_out[j - 1] = total.astype(bf16)
        direct[j] = send(back_out.at[j - 1], back_in.at[j - 1], y_peer[j])
    other, summed = back_term(1 - xl, 0), back_term(xl, 0)
    for number, j in enumerate(y_near):
        direct[j].wait_recv()
        other = other + beside_in[number, 0].astype(f32)
        summed = summed + beside_in[number, 1].astype(f32)
    back_edge_out[ny - 1] = other.astype(bf16)
    edge = send(back_edge_out.at[ny - 1], back_edge_in.at[ny - 1], lo_partner)
    drain(before_back)

    for j in near_steps + far_steps:
        z_copies[j].wait_recv()
    total = z_terms[0]
    for z_at in range(1, nz):
        total = total + z_terms[z_at]
    finals[core, y] = total
    own = finals.at[core, y]
    y_copies = [send(own, own, y_peer[j]) for j in y_far]

    edge.wait_recv()
    summed = summed + back_edge_in[ny - 1].astype(f32)
    for copy in y_copies:
        copy.wait_recv()
    pair = send(finals.at[core], finals.at[core], sibling)

    for j in y_rest:
        direct[j].wait_recv()
        summed = summed + back_in[j - 1].astype(f32)
    grad_features_ref[...] = (scale * summed).astype(bf16)

    drain(len(started))
    pair.wait_recv()
    for core_at in (0, 1):
        for y_at in range(ny):
            first = (core_at * ny + y_at) * chunk
            grad_weight_ref[first : first + chunk, :] = finals[core_at, y_at, :, :256]
    grad_bias_ref[...] = finals[0, 0, 0:2, 256:]


def store(*refs):
    for number in range(4):
        refs[4 + number][...] = refs[number][...]


def copies_of(ny, nz):
    forward = (2 * ny - 1) + 2 * (nz // 3) + (nz - 4) + nz
    backward = nz + nz + 2 * nz + (ny - 2) + (ny - 1)
    weights = 1 + (ny - 1) + 3 + (nz - 1) + (ny - 1) + 1
    return forward + backward + weights


def on_device(features, node_scale, weight, bias, block_rows, block_cols, block_masks, out_grad):
    ny, nz = lax.axis_size("row") // 2, lax.axis_size("col") // 4
    slots = block_masks.shape[2]
    bf16, f32, i32 = jnp.bfloat16, jnp.float32, jnp.int32
    chunk = weight.shape[0] // (2 * ny)
    block = (128, 128)
    anywhere = pl.BlockSpec(memory_space=pl.ANY)
    vmem = pl.BlockSpec(memory_space=pltpu.VMEM)
    copies = copies_of(ny, nz)
    results = (
        jax.ShapeDtypeStruct((128, 256), bf16),
        jax.ShapeDtypeStruct(block, bf16),
        jax.ShapeDtypeStruct((128, 256), f32),
        jax.ShapeDtypeStruct((2, 128), f32),
    )
    outs = pl.pallas_call(
        functools.partial(kernel, ny, nz),
        out_shape=results,
        in_specs=[anywhere] * 8,
        out_specs=(vmem,) * 4,
        scratch_shapes=[
            pltpu.VMEM(block, bf16),
            pltpu.VMEM((1, 128), bf16),
            pltpu.VMEM((128, 256), bf16),
            pltpu.VMEM((1, 256), f32),
            pltpu.SMEM((1, 1, slots), i32),
            pltpu.SMEM((1, 1, slots), i32),
            pltpu.VMEM((1, 1, slots) + block, i32),
            pltpu.VMEM((128, 256), bf16),
            pltpu.SMEM((slots,), i32),
            pltpu.SMEM((slots,), i32),
            pltpu.SMEM((2 * ny,), i32),
            pltpu.SMEM((4 * nz,), i32),
            pltpu.VMEM((slots,) + block, bf16),
            pltpu.VMEM((slots,) + block, bf16),
            pltpu.VMEM((2 * ny,) + block, bf16),
            pltpu.VMEM((slots + 1,) + block, f32),
            pltpu.VMEM((2, nz) + block, bf16),
            pltpu.VMEM((2, nz) + block, bf16),
            pltpu.VMEM((4, 2) + block, bf16),
            pltpu.VMEM((4, 2) + block, bf16),
            pltpu.VMEM((nz,) + block, bf16),
            pltpu.VMEM((nz,) + block, bf16),
            pltpu.VMEM((nz - 1,) + block, bf16),
            pltpu.VMEM((nz - 1,) + block, bf16),
            pltpu.VMEM((4 * nz,) + block, bf16),
            pltpu.VMEM((slots + 1,) + block, f32),
            pltpu.VMEM((2, 2) + block, bf16),
            pltpu.VMEM((2, 2) + block, bf16),
            pltpu.VMEM((ny,) + block, bf16),
            pltpu.VMEM((ny,) + block, bf16),
            pltpu.VMEM((ny - 1,) + block, bf16),
            pltpu.VMEM((ny - 1,) + block, bf16),
            pltpu.VMEM((2, ny, chunk, 384), f32),
            pltpu.VMEM((ny, chunk, 384), f32),
            pltpu.VMEM((ny, chunk, 384), f32),
            pltpu.VMEM((ny - 1, chunk, 384), f32),
            pltpu.VMEM((4, chunk, 384), f32),
            pltpu.VMEM((nz, chunk, 384), f32),
            pltpu.VMEM((2, ny, chunk, 384), f32),
            pltpu.SemaphoreType.DMA((8,)),
            pltpu.SemaphoreType.DMA((copies,)),
            pltpu.SemaphoreType.DMA((copies,)),
        ],
        compiler_params=pltpu.CompilerParams(
            collective_id=0, has_side_effects=True, vmem_limit_bytes=60 * 1024 * 1024
        ),
        cost_estimate=pl.CostEstimate(
            flops=200_000_000, bytes_accessed=2_000_000, transcendentals=32768
        ),
    )(
        features, node_scale.reshape(1, 128), weight, bias.reshape(1, 256),
        block_rows, block_cols, block_masks, out_grad,
    )
    hidden, grad_features, grad_weight, grad_bias = pl.pallas_call(
        store,
        out_shape=results,
        in_specs=[vmem] * 4,
        out_specs=(vmem,) * 4,
    )(*outs)
    return hidden, grad_features, grad_weight, grad_bias.reshape(256)


def solution(mesh):
    return jax.shard_map(
        on_device,
        mesh=mesh,
        in_specs=(
            P(("row", "col"), None),
            P(("row", "col")),
            P(),
            P(),
            P("row", "col", None),
            P("row", "col", None),
            P("row", "col", None, None, None),
            P(("row", "col"), None),
        ),
        out_specs=(P(("row", "col"), None), P(("row", "col"), None), P(), P()),
        check_vma=False,
    )
```

```python
import functools
import math

import jax
import jax.numpy as jnp
from jax import lax
from jax.experimental import pallas as pl
from jax.experimental.pallas import tpu as pltpu
from jax.sharding import PartitionSpec as P

MESH = pl.DeviceIdType.MESH


def far_first(count):
    return sorted(range(1, count), key=lambda step: -min(step, count - step))


def kernel(
    ny, nz,
    features_hbm, scale_hbm, weight_hbm, bias_hbm, rows_hbm, cols_hbm, masks_hbm, cotangent_hbm,
    hidden_ref, grad_features_ref, grad_weight_ref, grad_bias_ref,
    features_ref, scale_ref, weight_ref, bias_ref, row_ids, col_ids, masks_ref, cotangent_ref,
    message_ids, earlier, last, owners,
    masks, masks_t, gathered, products, pair_out, pair_in, near_out, near_in, edge_out, edge_in, ring_out, ring_in,
    messages, back, beside_out, beside_in, back_edge_out, back_edge_in, back_out, back_in,
    parts, parts_in, halves, y_in, x_terms, z_terms, finals,
    load_sems, send_sems, recv_sems,
):
    f32, bf16 = jnp.float32, jnp.bfloat16
    slots = masks.shape[0]
    row, col = lax.axis_index("row"), lax.axis_index("col")
    xl, y = row // ny, row % ny
    xh, z, core = col // (2 * nz), (col % (2 * nz)) // 2, col % 2

    def row_of(x_lo, y_at):
        return x_lo * ny + y_at

    def col_of(x_hi, z_at, core_at):
        return x_hi * (2 * nz) + z_at * 2 + core_at

    sibling = (row, col_of(xh, z, 1 - core))
    lo_partner = (row_of(1 - xl, y), col)
    hi_partner = (row, col_of(1 - xh, z, core))
    far_partner = (row_of(1 - xl, y), col_of(1 - xh, z, core))
    y_far, z_far = far_first(ny), far_first(nz)
    y_peer = {j: (row_of(xl, (y + j) % ny), col) for j in y_far}
    reach = nz // 4
    ends = (reach, nz - reach)
    far_steps = [j for j in z_far if reach < j < nz - reach]
    near_steps = [j for j in z_far if j not in far_steps and j not in ends]
    z_peer = {
        j: (row, col_of(xh, (z + j) % nz, core)) for j in list(ends) + near_steps
    }

    barrier = pltpu.get_barrier_semaphore()
    everyone = [sibling, lo_partner, hi_partner, far_partner]
    everyone = [y_peer[j] for j in y_far] + list(z_peer.values()) + everyone
    for peer in everyone:
        pl.semaphore_signal(barrier, inc=1, device_id=peer, device_id_type=MESH)

    loads = []
    for number, (src, dst) in enumerate((
        (features_hbm, features_ref), (scale_hbm, scale_ref), (rows_hbm, row_ids),
        (cols_hbm, col_ids), (masks_hbm, masks_ref), (weight_hbm, weight_ref),
        (bias_hbm, bias_ref), (cotangent_hbm, cotangent_ref),
    )):
        load = pltpu.make_async_copy(src, dst, load_sems.at[number])
        load.start()
        loads.append(load)

    started = []

    def send(src, dst, peer):
        number = len(started)
        copy = pltpu.make_async_remote_copy(
            src_ref=src, dst_ref=dst, send_sem=send_sems.at[number], recv_sem=recv_sems.at[number],
            device_id=peer, device_id_type=MESH,
        )
        started.append(copy)
        copy.start()
        return copy

    drained = []

    def drain(count):
        for copy in started[len(drained) : count]:
            copy.wait_send()
            drained.append(copy)

    loads[0].wait()
    loads[1].wait()
    scale = jnp.broadcast_to(scale_ref[...].astype(f32), (128, 128)).T
    gathered[row] = (scale * features_ref[...].astype(f32)).astype(bf16)
    pl.semaphore_wait(barrier, len(everyone))

    own = gathered.at[row]
    direct = {j: send(own, own, y_peer[j]) for j in y_far}
    swapped = [send(own, own, lo_partner)]

    for load in loads[2:5]:
        load.wait()
    def find_owner(place, carry):
        found = slots
        for slot in range(slots):
            found = jnp.where(row_ids[0, 0, slot] == place, slot, found)
        owners[place] = found
        return carry

    def prepare(slot, carry):
        masks[slot] = masks_ref[0, 0, slot].astype(f32).astype(bf16)
        return carry

    lax.fori_loop(0, slots, prepare, 0)
    swapped[0].wait_recv()
    other = gathered.at[row_of(1 - xl, y)]
    crossed = [send(other, other, y_peer[j]) for j in (1, ny - 1)]
    products[slots] = jnp.zeros((128, 128), f32)

    for j in y_far:
        direct[j].wait_recv()
        if j not in (1, ny - 1):
            block = gathered.at[row_of(xl, (y - j) % ny)]
            swapped.append(send(block, block, lo_partner))
    lax.fori_loop(0, 4 * nz, find_owner, 0)
    for copy in swapped[1:] + crossed:
        copy.wait_recv()

    for slot in range(slots):
        products[slot] = jnp.dot(
            masks[slot], gathered[col_ids[0, 0, slot]], preferred_element_type=f32
        )

    def term(x_hi, j, core_at):
        return products[owners[col_of(x_hi, (z + j) % nz, core_at)]]

    z_order = z_far + [0]
    group = 2
    pair_copies = {}
    for piece, x_hi in enumerate((1 - xh, xh)):
        for place, j in enumerate(z_order):
            pair_out[piece, place] = term(x_hi, j, 1 - core).astype(bf16)
            if place % group == group - 1:
                span = pl.ds(place - group + 1, group)
                pair_copies[piece, place // group] = send(
                    pair_out.at[piece, span], pair_in.at[piece, span], sibling
                )
    taken = set()

    def pair_sum(piece, j):
        place = z_order.index(j)
        if (piece, place // group) not in taken:
            taken.add((piece, place // group))
            pair_copies[piece, place // group].wait_recv()
        x_hi = 1 - xh if piece == 0 else xh
        return term(x_hi, j, core) + pair_in[piece, place].astype(f32)

    edges = {}
    for place, j in enumerate(far_steps + list(ends)):
        edge_out[place] = pair_sum(0, j).astype(bf16)
        edges[j] = send(edge_out.at[place], edge_in.at[place], hi_partner)
    direct, relayed = {}, {}
    for number, j in enumerate(near_steps):
        near_out[number, 0] = pair_sum(0, j).astype(bf16)
        near_out[number, 1] = pair_sum(1, j).astype(bf16)
        direct[j] = send(near_out.at[number], near_in.at[number], z_peer[j])
    half = pl.ds(0, 64), pl.ds(64, 64)

    def far_sum(j):
        total = pair_sum(1, j)
        edges[j].wait_recv()
        return total + edge_in[(far_steps + list(ends)).index(j)].astype(f32)

    for j in far_steps:
        ring_out[j - 1] = far_sum(j).astype(bf16)
        if 2 * j == nz:
            for way, hop in enumerate(ends):
                relayed[j, way] = send(
                    ring_out.at[j - 1, half[way]], ring_in.at[j - 1, half[way]], z_peer[hop]
                )
        else:
            hop = j - reach if 2 * j < nz else j + reach
            relayed[j] = send(ring_out.at[j - 1], ring_in.at[j - 1], z_peer[hop])
    relay_sums = {j: far_sum(j) for j in ends}
    other, summed = pair_sum(0, 0), pair_sum(1, 0)
    for number, j in enumerate(near_steps):
        direct[j].wait_recv()
        other = other + near_in[number, 0].astype(f32)
        summed = summed + near_in[number, 1].astype(f32)
    edge_out[nz - 1] = other.astype(bf16)
    edges[0] = send(edge_out.at[nz - 1], edge_in.at[nz - 1], hi_partner)
    for way, j in enumerate(ends):
        total = relay_sums[j]
        for far in far_steps:
            if 2 * far != nz and (2 * far < nz) == (way == 0):
                relayed[far].wait_recv()
                total = total + ring_in[far - 1].astype(f32)
        relayed[nz // 2, way].wait_recv()
        middle = ring_in[nz // 2 - 1, 64 * way : 64 * way + 64, :].astype(f32)
        if way == 0:
            ring_out[j - 1, :64, :] = (total[:64] + middle).astype(bf16)
            ring_out[j - 1, 64:, :] = total[64:].astype(bf16)
        else:
            ring_out[j - 1, :64, :] = total[:64].astype(bf16)
            ring_out[j - 1, 64:, :] = (total[64:] + middle).astype(bf16)
        direct[j] = send(ring_out.at[j - 1], ring_in.at[j - 1], z_peer[j])

    for slot in range(slots):
        row_id = row_ids[0, 0, slot]
        message_ids[slot] = (
            (row_id % 2) * (2 * nz) + (row_id // (2 * nz)) * nz + (row_id % (2 * nz)) // 2
        )
        found = slots
        for other in range(slot):
            found = jnp.where(col_ids[0, 0, other] == col_ids[0, 0, slot], other, found)
        earlier[slot] = found

    def find_last(place, carry):
        found = slots
        for slot in range(slots):
            found = jnp.where(col_ids[0, 0, slot] == place, slot, found)
        last[place] = found
        return carry

    def transpose(slot, carry):
        masks_t[slot] = masks_ref[0, 0, slot].astype(f32).T.astype(bf16)
        return carry

    lax.fori_loop(0, 2 * ny, find_last, 0)
    lax.fori_loop(0, slots, transpose, 0)
    back[slots] = jnp.zeros((128, 128), f32)
    for load in loads[5:]:
        load.wait()
    edges[0].wait_recv()
    summed = summed + edge_in[nz - 1].astype(f32)
    for j in ends:
        direct[j].wait_recv()
        summed = summed + ring_in[j - 1].astype(f32)

    aggregated = (scale * summed).astype(bf16)
    weight = weight_ref[...]
    preact = jnp.dot(aggregated, weight, preferred_element_type=f32) + bias_ref[...]
    root = math.sqrt(2.0 / math.pi)
    square = preact * preact
    slope = jnp.tanh(root * (preact + 0.044715 * (square * preact)))
    cdf = 0.5 * (1.0 + slope)
    derivative = cdf + preact * (0.5 * (1.0 - slope * slope) * (root * (1.0 + 0.134145 * square)))
    grad_pre = (cotangent_ref[...].astype(f32) * derivative).astype(bf16)
    message = scale * lax.dot_general(
        grad_pre, weight, (((1,), (1,)), ((), ())), preferred_element_type=f32
    )

    before_messages = len(started)
    shared = []

    def message_at(x_hi, z_at):
        return messages.at[(core * 2 + x_hi) * nz + z_at]

    def share(block):
        shared.append(send(block, block, sibling))

    messages[(core * 2 + xh) * nz + z] = message.astype(bf16)
    own = message_at(xh, z)
    direct = {j: send(own, own, z_peer[j]) for j in ends}
    swapped = {0: send(own, own, hi_partner)}
    for j in near_steps:
        direct[j] = send(own, own, z_peer[j])
    share(own)

    chunk = parts.shape[2]

    hidden_ref[...] = (preact * cdf).astype(bf16)
    weight_part = lax.dot_general(
        aggregated, grad_pre, (((0,), (0,)), ((), ())), preferred_element_type=f32
    )
    bias_part = jnp.sum(grad_pre.astype(f32), axis=0, keepdims=True)
    lines = lax.broadcasted_iota(jnp.int32, (chunk, 128), 0)
    bias_tile = jnp.where(
        lines == 0, bias_part[:, :128], jnp.where(lines == 1, bias_part[:, 128:], 0.0)
    )
    for core_at in (0, 1):
        for y_at in range(ny):
            first = (core_at * ny + y_at) * chunk
            parts[core_at, y_at, :, :256] = weight_part[first : first + chunk]
            parts[core_at, y_at, :, 256:] = bias_tile
    pair = send(parts.at[1 - core], parts_in, sibling)
    drain(before_messages)
    def pass_on(j):
        block = message_at(xh, (z - j) % nz)
        swapped[j] = send(block, block, hi_partner)
        share(block)

    relayed = {}
    for way, j in enumerate(ends):
        direct[j].wait_recv()
        place = (core * 2 + xh) * nz + (z - j) % nz
        for hop in range(reach, 0, -1):
            far = reach + hop if way == 0 else nz - reach - hop
            peer = z_peer[hop if way == 0 else nz - hop]
            if hop == reach:
                part = messages.at[place, half[way]]
                relayed[far, way] = send(part, part, peer)
            else:
                part = messages.at[place]
                relayed[far] = send(part, part, peer)
        pass_on(j)
    for j in near_steps:
        direct[j].wait_recv()
        pass_on(j)

    pair.wait_recv()
    halves[...] = parts[core] + parts_in[...]
    y_copies = {j: send(halves.at[(y + j) % ny], y_in.at[j - 1], y_peer[j]) for j in y_far}

    for j in far_steps[::-1]:
        if 2 * j == nz:
            relayed[j, 0].wait_recv()
            relayed[j, 1].wait_recv()
        else:
            relayed[j].wait_recv()
        pass_on(j)

    order = [0, reach, nz - reach] + near_steps
    for j in order:
        swapped[j].wait_recv()
        share(message_at(1 - xh, (z - j) % nz))

    total = halves[y]
    for j in y_far:
        y_copies[j].wait_recv()
        total = total + y_in[j - 1]
    x_at = xh * 2 + xl
    x_terms[x_at] = total
    x_copies = [
        send(x_terms.at[x_at], x_terms.at[x_at], peer)
        for peer in (lo_partner, hi_partner, far_partner)
    ]

    for j in far_steps[::-1]:
        swapped[j].wait_recv()
        share(message_at(1 - xh, (z - j) % nz))

    for copy in x_copies:
        copy.wait_recv()
    z_terms[z] = (x_terms[0] + x_terms[1]) + (x_terms[2] + x_terms[3])
    own = z_terms.at[z]
    z_copies = {j: send(own, own, z_peer[j]) for j in list(ends) + near_steps}

    for copy in shared:
        copy.wait_recv()

    before_back = len(started)
    for slot in range(slots):
        product = jnp.dot(
            masks_t[slot], messages[message_ids[slot]], preferred_element_type=f32
        )
        back[slot] = product + back[earlier[slot]]

    def back_term(x_lo, j):
        return back[last[row_of(x_lo, (y + j) % ny)]]

    y_near = (1, ny - 1)
    y_rest = [j for j in y_far if j not in y_near]
    edges, direct = {}, {}
    for place, j in enumerate(y_rest):
        back_edge_out[place] = back_term(1 - xl, j).astype(bf16)
        edges[j] = send(back_edge_out.at[place], back_edge_in.at[place], lo_partner)
    for number, j in enumerate(y_near):
        beside_out[number, 0] = back_term(1 - xl, j).astype(bf16)
        beside_out[number, 1] = back_term(xl, j).astype(bf16)
        direct[j] = send(beside_out.at[number], beside_in.at[number], y_peer[j])
    for way, j in enumerate(ends):
        z_copies[j].wait_recv()
        block = z_terms.at[(z - j) % nz]
        for hop in range(reach - way, 0, -1):
            far = reach + hop if way == 0 else nz - reach - hop
            z_copies[far] = send(block, block, z_peer[hop if way == 0 else nz - hop])
    for place, j in enumerate(y_rest):
        total = back_term(xl, j)
        edges[j].wait_recv()
        total = total + back_edge_in[place].astype(f32)
        back_out[j - 1] = total.astype(bf16)
        direct[j] = send(back_out.at[j - 1], back_in.at[j - 1], y_peer[j])
    other, summed = back_term(1 - xl, 0), back_term(xl, 0)
    for number, j in enumerate(y_near):
        direct[j].wait_recv()
        other = other + beside_in[number, 0].astype(f32)
        summed = summed + beside_in[number, 1].astype(f32)
    back_edge_out[ny - 1] = other.astype(bf16)
    edge = send(back_edge_out.at[ny - 1], back_edge_in.at[ny - 1], lo_partner)
    drain(before_back)

    for j in near_steps + far_steps:
        z_copies[j].wait_recv()
    total = z_terms[0]
    for z_at in range(1, nz):
        total = total + z_terms[z_at]
    finals[core, y] = total
    own = finals.at[core, y]
    y_copies = [send(own, own, y_peer[j]) for j in y_far]

    edge.wait_recv()
    summed = summed + back_edge_in[ny - 1].astype(f32)
    for j in y_rest:
        direct[j].wait_recv()
        summed = summed + back_in[j - 1].astype(f32)
    grad_features_ref[...] = (scale * summed).astype(bf16)

    for copy in y_copies:
        copy.wait_recv()
    pair = send(finals.at[core], finals.at[core], sibling)
    drain(len(started))
    pair.wait_recv()
    for core_at in (0, 1):
        for y_at in range(ny):
            first = (core_at * ny + y_at) * chunk
            grad_weight_ref[first : first + chunk, :] = finals[core_at, y_at, :, :256]
    grad_bias_ref[...] = finals[0, 0, 0:2, 256:]


def store(*refs):
    for number in range(4):
        refs[4 + number][...] = refs[number][...]


def copies_of(ny, nz):
    forward = (2 * ny - 1) + 2 * (nz // 2) + (nz - 4) + nz
    backward = nz + nz + 2 * nz + (ny - 2) + (ny - 1)
    weights = 1 + (ny - 1) + 3 + (nz - 1) + (ny - 1) + 1
    return forward + backward + weights


def on_device(features, node_scale, weight, bias, block_rows, block_cols, block_masks, out_grad):
    ny, nz = lax.axis_size("row") // 2, lax.axis_size("col") // 4
    slots = block_masks.shape[2]
    bf16, f32, i32 = jnp.bfloat16, jnp.float32, jnp.int32
    chunk = weight.shape[0] // (2 * ny)
    block = (128, 128)
    anywhere = pl.BlockSpec(memory_space=pl.ANY)
    vmem = pl.BlockSpec(memory_space=pltpu.VMEM)
    copies = copies_of(ny, nz)
    results = (
        jax.ShapeDtypeStruct((128, 256), bf16),
        jax.ShapeDtypeStruct(block, bf16),
        jax.ShapeDtypeStruct((128, 256), f32),
        jax.ShapeDtypeStruct((2, 128), f32),
    )
    outs = pl.pallas_call(
        functools.partial(kernel, ny, nz),
        out_shape=results,
        in_specs=[anywhere] * 8,
        out_specs=(vmem,) * 4,
        scratch_shapes=[
            pltpu.VMEM(block, bf16),
            pltpu.VMEM((1, 128), bf16),
            pltpu.VMEM((128, 256), bf16),
            pltpu.VMEM((1, 256), f32),
            pltpu.SMEM((1, 1, slots), i32),
            pltpu.SMEM((1, 1, slots), i32),
            pltpu.VMEM((1, 1, slots) + block, i32),
            pltpu.VMEM((128, 256), bf16),
            pltpu.SMEM((slots,), i32),
            pltpu.SMEM((slots,), i32),
            pltpu.SMEM((2 * ny,), i32),
            pltpu.SMEM((4 * nz,), i32),
            pltpu.VMEM((slots,) + block, bf16),
            pltpu.VMEM((slots,) + block, bf16),
            pltpu.VMEM((2 * ny,) + block, bf16),
            pltpu.VMEM((slots + 1,) + block, f32),
            pltpu.VMEM((2, nz) + block, bf16),
            pltpu.VMEM((2, nz) + block, bf16),
            pltpu.VMEM((4, 2) + block, bf16),
            pltpu.VMEM((4, 2) + block, bf16),
            pltpu.VMEM((nz,) + block, bf16),
            pltpu.VMEM((nz,) + block, bf16),
            pltpu.VMEM((nz - 1,) + block, bf16),
            pltpu.VMEM((nz - 1,) + block, bf16),
            pltpu.VMEM((4 * nz,) + block, bf16),
            pltpu.VMEM((slots + 1,) + block, f32),
            pltpu.VMEM((2, 2) + block, bf16),
            pltpu.VMEM((2, 2) + block, bf16),
            pltpu.VMEM((ny,) + block, bf16),
            pltpu.VMEM((ny,) + block, bf16),
            pltpu.VMEM((ny - 1,) + block, bf16),
            pltpu.VMEM((ny - 1,) + block, bf16),
            pltpu.VMEM((2, ny, chunk, 384), f32),
            pltpu.VMEM((ny, chunk, 384), f32),
            pltpu.VMEM((ny, chunk, 384), f32),
            pltpu.VMEM((ny - 1, chunk, 384), f32),
            pltpu.VMEM((4, chunk, 384), f32),
            pltpu.VMEM((nz, chunk, 384), f32),
            pltpu.VMEM((2, ny, chunk, 384), f32),
            pltpu.SemaphoreType.DMA((8,)),
            pltpu.SemaphoreType.DMA((copies,)),
            pltpu.SemaphoreType.DMA((copies,)),
        ],
        compiler_params=pltpu.CompilerParams(
            collective_id=0, has_side_effects=True, vmem_limit_bytes=60 * 1024 * 1024
        ),
        cost_estimate=pl.CostEstimate(
            flops=200_000_000, bytes_accessed=2_000_000, transcendentals=32768
        ),
    )(
        features, node_scale.reshape(1, 128), weight, bias.reshape(1, 256),
        block_rows, block_cols, block_masks, out_grad,
    )
    hidden, grad_features, grad_weight, grad_bias = pl.pallas_call(
        store,
        out_shape=results,
        in_specs=[vmem] * 4,
        out_specs=(vmem,) * 4,
    )(*outs)
    return hidden, grad_features, grad_weight, grad_bias.reshape(256)


def solution(mesh):
    return jax.shard_map(
        on_device,
        mesh=mesh,
        in_specs=(
            P(("row", "col"), None),
            P(("row", "col")),
            P(),
            P(),
            P("row", "col", None),
            P("row", "col", None),
            P("row", "col", None, None, None),
            P(("row", "col"), None),
        ),
        out_specs=(P(("row", "col"), None), P(("row", "col"), None), P(), P()),
        check_vma=False,
    )
```
